128 devices in a mesh: dp: 4 (over z), feat: 32 (over y, x, core).
Axes of the slice: x: 4, y: 4, z: 4, core: 2. Of those that a mesh axis runs over, the one named last changes fastest.
Arguments:
- acts: bfloat16 [24576, 768], P(('dp', 'feat')), may hold values from -6 to 6
- valid: int32 [24576], P(('dp', 'feat')), may hold values from 0 to 1, as said below
- enc_master: float32 [768, 24576], P(None, 'feat'), may hold values from -0.21875 to 0.21875
- enc_bias: float32 [24576], P('feat'), may hold values from -4 to -2
- dec_master: float32 [24576, 768], P('feat'), may hold values from -0.21875 to 0.21875
- dec_bias: float32 [768], replicated, may hold values from -1.5 to 1.5
- enc_moment: float32 [768, 24576], P(None, 'feat'), may hold values from -0.1 to 0.1
- enc_bias_moment: float32 [24576], P('feat'), may hold values from -0.35 to 0.35
- dec_moment: float32 [24576, 768], P('feat'), may hold values from -0.25 to 0.25
- dec_bias_moment: float32 [768], replicated, may hold values from -5 to 5
- enc_average: float32 [768, 24576], P(None, 'feat'), may hold values from -0.21875 to 0.21875
- enc_bias_average: float32 [24576], P('feat'), may hold values from -4 to -2
- dec_average: float32 [24576, 768], P('feat'), may hold values from -0.21875 to 0.21875
- dec_bias_average: float32 [768], replicated, may hold values from -1.5 to 1.5
Outputs:
- loss_sum: float32 [], replicated
- count: float32 [], replicated
- enc_new: float32 [768, 24576], P(None, 'feat')
- enc_bias_new: float32 [24576], P('feat')
- dec_new: float32 [24576, 768], P('feat')
- dec_bias_new: float32 [768], replicated
- enc_moment_new: float32 [768, 24576], P(None, 'feat')
- enc_bias_moment_new: float32 [24576], P('feat')
- dec_moment_new: float32 [24576, 768], P('feat')
- dec_bias_moment_new: float32 [768], replicated
- enc_average_new: float32 [768, 24576], P(None, 'feat')
- enc_bias_average_new: float32 [24576], P('feat')
- dec_average_new: float32 [24576, 768], P('feat')
- dec_bias_average_new: float32 [768], replicated
The draws below stay inside these ranges and needn't reach their ends.
Inputs may be any that keep to these rules, and one draw needn't show every extreme that they name: `valid`: 0 at every position that is a multiple of 128.
All inputs are finite; a program needn't handle non-finite values.
Results may differ from the reference program's by a relative error of at most 0.008.
Values may be sent and summed in bfloat16 or wider, within the bound.
No kernel may reach another device: no remote copies, remote signals or barrier semaphores. Data moves between devices by JAX's collectives and lax.ppermute only.
A program may use at most 192 MiB of HBM per device.

```python
import math
import jax
import jax.numpy as jnp
from jax import lax

HEADS = 12
HEAD = 64
F = 24576
CONTEXT = 128
D = 768
TOKENS = 24576
N_FEAT = 32


def draw_valid(key, part):
    key = jax.random.fold_in(key, 7)
    key_roll, key_shift, key_sign, key_jitter, key_jsign = jax.random.split(key, 5)
    position = jnp.arange(TOKENS, dtype=jnp.int32)
    quarter = 4 * position // TOKENS
    shift = jax.random.randint(key_shift, (), 80, 151, dtype=jnp.int32)
    shift = shift * (2 * jax.random.randint(key_sign, (), 0, 2, dtype=jnp.int32) - 1)
    jitter = jax.random.randint(key_jitter, (4,), 40, 81, dtype=jnp.int32)
    jitter = jitter * (2 * jax.random.randint(key_jsign, (4,), 0, 2, dtype=jnp.int32) - 1)
    level = 300 + 500 * position // TOKENS + shift + jitter[quarter]
    roll = jax.random.randint(key_roll, (TOKENS,), 0, 1000, dtype=jnp.int32)
    keep = (roll < level) & (position % CONTEXT != 0)
    return keep.astype(jnp.int32)


def block_levels(rng, extent, cuts, low, largest):
    factor_of = 1.0
    for dim, shards_of in cuts:
        steps = jax.random.uniform(jax.random.fold_in(jax.random.fold_in(rng, 6), dim), (shards_of,), jnp.float32, low / len(cuts), largest / len(cuts))
        factor_of = factor_of * jnp.repeat(jnp.exp(steps), extent[dim] // shards_of).reshape((-1,) + (1,) * (len(extent) - 1 - dim))
    return factor_of


def centred(key, dims, spread, reach, cuts=(), held_as=jnp.bfloat16):
    result = spread * jax.random.normal(key, dims, jnp.float32)
    if cuts:
        result = result * block_levels(key, dims, cuts, -0.22, 0.18)
    return jnp.clip(result, -reach, reach).astype(held_as)


def setup_inputs(seed: int = 0) -> dict:
    arg_keys = jax.random.split(jax.random.key(seed), 15)
    acts = centred(arg_keys[0], (TOKENS, D), 1.0, 6.0, ((0, 128),))
    valid = draw_valid(jax.random.fold_in(arg_keys[14], 71), 0)
    enc_master = centred(arg_keys[2], (D, F), D ** -0.5, 0.21875, ((1, 32),), jnp.float32)
    enc_bias = jnp.clip(-4.0 + 2.0 * jax.random.uniform(arg_keys[3], (F,), jnp.float32) ** block_levels(arg_keys[3], (F,), ((0, 32),), -0.2, 0.2), -4.0, -2.0)
    dec_master = centred(arg_keys[4], (F, D), D ** -0.5, 0.21875, ((0, 32),), jnp.float32)
    dec_bias = centred(arg_keys[5], (D,), 0.3, 1.5, (), jnp.float32)
    enc_moment = centred(arg_keys[6], (D, F), 0.02, 0.1, ((1, 32),), jnp.float32)
    enc_bias_moment = centred(arg_keys[7], (F,), 0.07, 0.35, ((0, 32),), jnp.float32)
    dec_moment = centred(arg_keys[8], (F, D), 0.05, 0.25, ((0, 32),), jnp.float32)
    dec_bias_moment = centred(arg_keys[9], (D,), 1.0, 5.0, (), jnp.float32)
    enc_average = centred(arg_keys[10], (D, F), D ** -0.5, 0.21875, ((1, 32),), jnp.float32)
    enc_bias_average = jnp.clip(-4.0 + 2.0 * jax.random.uniform(arg_keys[11], (F,), jnp.float32) ** block_levels(arg_keys[11], (F,), ((0, 32),), -0.2, 0.2), -4.0, -2.0)
    dec_average = centred(arg_keys[12], (F, D), D ** -0.5, 0.21875, ((0, 32),), jnp.float32)
    dec_bias_average = centred(arg_keys[13], (D,), 0.3, 1.5, (), jnp.float32)
    return dict(acts=acts, valid=valid, enc_master=enc_master, enc_bias=enc_bias, dec_master=dec_master, dec_bias=dec_bias, enc_moment=enc_moment, enc_bias_moment=enc_bias_moment, dec_moment=dec_moment, dec_bias_moment=dec_bias_moment, enc_average=enc_average, enc_bias_average=enc_bias_average, dec_average=dec_average, dec_bias_average=dec_bias_average)


sparsity_cost = 0.2
momentum_rate = 0.9
average_rate = 0.8

@jax.custom_vjp
def low(v):
    return lax.optimization_barrier(v.astype(jnp.bfloat16)).astype(jnp.float32)

@jax.custom_vjp
def low_back(v):
    return v

def low_keep(v):
    return (low(v), None)

def low_pass(kept, grad):
    return (grad,)

def back_keep(v):
    return (v, None)

def back_low(kept, grad):
    return (low(grad),)
low.defvjp(low_keep, low_pass)
low_back.defvjp(back_keep, back_low)

def head_weights(width):
    return 0.5 + (jnp.arange(width) // HEAD).astype(jnp.float32) / (HEADS - 1)

def advance(master, moment, average, grad, rate, rows_unit):
    moment_new = momentum_rate * moment + grad
    master_new = master - rate * (grad + momentum_rate * moment_new)
    if rows_unit:
        master_new = master_new * lax.rsqrt(lax.optimization_barrier(jnp.sum(master_new * master_new, axis=1, keepdims=True)) + 1e-06)
    return (master_new, moment_new, average_rate * average + (1.0 - average_rate) * master_new)

def reference(acts, valid, enc_master, enc_bias, dec_master, dec_bias, enc_moment, enc_bias_moment, dec_moment, dec_bias_moment, enc_average, enc_bias_average, dec_average, dec_bias_average):
    inputs = acts.astype(jnp.float32)
    flags = valid.astype(jnp.float32)
    count = jnp.sum(flags)
    width = inputs.shape[1]
    weight = head_weights(width)
    block = math.gcd(TOKENS, 1024)
    blocks = TOKENS // block
    input_blocks = inputs.reshape(blocks, block, width)
    flag_blocks = flags.reshape(blocks, block)
    highest = lax.Precision.HIGHEST
    shard_feats = F // N_FEAT

    def loss_fn(params):
        enc_w, enc_b, dec_w, dec_b = params
        enc_low = low(enc_w)
        dec_low = low(dec_w)
        dec_groups = dec_low.reshape(N_FEAT, shard_feats, width)

        @jax.checkpoint
        def block_loss(rows, marks):
            centered = low(rows - dec_b)
            pre = low_back(jnp.dot(centered, enc_low, precision=highest)) + enc_b
            feats = jax.nn.softplus(pre)
            feat_groups = low(feats).reshape(rows.shape[0], N_FEAT, shard_feats)
            partial_value = jnp.einsum('bsf,sfd->bsd', feat_groups, dec_groups, precision=highest)
            decoded = low_back(lax.optimization_barrier(jnp.sum(low(partial_value), axis=1)))
            err = decoded + dec_b - rows
            square = jnp.sum(marks[:, None] * weight * err * err)
            return square + sparsity_cost * jnp.sum(marks[:, None] * feats)

        def step(total, item):
            return (total + block_loss(item[0], item[1]), None)
        total, _ = lax.scan(step, jnp.zeros((), jnp.float32), (input_blocks, flag_blocks))
        return total
    loss_sum, pull = jax.vjp(loss_fn, (enc_master, enc_bias, dec_master, dec_bias))
    (g_enc, g_enc_bias, g_dec, g_dec_bias), = pull(1.0 / count)
    enc_new, enc_moment_new, enc_average_new = advance(enc_master, enc_moment, enc_average, g_enc, 0.3, False)
    enc_bias_new, enc_bias_moment_new, enc_bias_average_new = advance(enc_bias, enc_bias_moment, enc_bias_average, g_enc_bias, 2.0, False)
    dec_new, dec_moment_new, dec_average_new = advance(dec_master, dec_moment, dec_average, g_dec, 0.3, True)
    dec_bias_new, dec_bias_moment_new, dec_bias_average_new = advance(dec_bias, dec_bias_moment, dec_bias_average, g_dec_bias, 0.1, False)
    return (loss_sum, count, enc_new, enc_bias_new, dec_new, dec_bias_new, enc_moment_new, enc_bias_moment_new, dec_moment_new, dec_bias_moment_new, enc_average_new, enc_bias_average_new, dec_average_new, dec_bias_average_new)
```

```python
import functools
import itertools

import jax
import jax.numpy as jnp
from jax import lax
from jax.experimental import pallas as pl
from jax.experimental.pallas import tpu as pltpu
from jax.sharding import PartitionSpec as P

HEAD = 64
F32 = jnp.float32
BF = jnp.bfloat16

sparsity_cost = 0.2
momentum_rate = 0.9
average_rate = 0.8

AXES = ("dp", "feat")
SENTINEL = 1000.0
TN = (((0,), (0,)), ((), ()))
NT = (((1,), (1,)), ((), ()))


def step_pairs(first, second, shift):
    pairs = []
    for z, y, x, c in itertools.product(range(4), range(4), range(4), range(2)):
        at = {"z": z, "y": y, "x": x}
        axis = first if c == 0 else second
        to = dict(at)
        to[axis] = (at[axis] + shift) % 4
        pairs.append((((z * 4 + y) * 4 + x) * 2 + c, ((to["z"] * 4 + to["y"]) * 4 + to["x"]) * 2 + c))
    return pairs


def move(v, axes, shift):
    return lax.ppermute(v, AXES, step_pairs(axes[0], axes[1], shift))


def swap(v, bit):
    return lax.ppermute(v, AXES, [(i, i ^ bit) for i in range(128)])


INNER = ("x", "y")
OUTER = ("y", "x")
DEPTH = ("z", "z")


def ring_gather(block, axes):
    half = block.shape[0] // 2
    p = move(block, axes, 1)
    m = move(block, axes, 3)
    top = move(p[:half], axes, 1)
    bottom = move(m[half:], axes, 3)
    return p, m, top, bottom


def ring_scatter(own, p, m, far_top, far_bottom, axes):
    half = p.shape[0] // 2
    r_top = move(far_top.astype(BF), axes, 3)
    r_bottom = move(far_bottom.astype(BF), axes, 1)
    p = p.astype(F32)
    m = m.astype(F32)
    p_sum = jnp.concatenate([p[:half] + r_top.astype(F32), p[half:]], 0).astype(BF)
    m_sum = jnp.concatenate([m[:half], m[half:] + r_bottom.astype(F32)], 0).astype(BF)
    a = move(p_sum, axes, 3)
    b = move(m_sum, axes, 1)
    return own.astype(F32) + a.astype(F32) + b.astype(F32)


def params():
    return pltpu.CompilerParams(dimension_semantics=("arbitrary",), vmem_limit_bytes=56 * 2**20)


def activate(pre):
    t = jnp.exp(-jnp.abs(pre))
    u = 1.0 + t
    feats = jnp.maximum(pre, 0.0) + jnp.where(t < 1e-3, t * (1.0 - 0.5 * t), jnp.log(u))
    r = 1.0 / u
    return feats, jnp.where(pre >= 0, r, t * r)


def encode_body(fc, c_ref, enc_ref, b_ref, dec_ref, f_ref, s_ref, p_ref, sp_ref):
    c = c_ref[...]
    off = jnp.where(c[:, 0:1].astype(F32) > 0.5 * SENTINEL, -1e30, 0.0)
    acc = tot = None
    for k in range(enc_ref.shape[1] // fc):
        sl = slice(k * fc, (k + 1) * fc)
        pre = jnp.dot(c, enc_ref[:, sl], preferred_element_type=F32) + b_ref[:, sl] + off
        feats, sig = activate(pre)
        low = feats.astype(BF)
        f_ref[:, sl] = low
        s_ref[:, sl] = sig.astype(BF)
        d = jnp.dot(low, dec_ref[sl, :], preferred_element_type=F32)
        acc = d if acc is None else acc + d
        part = jnp.sum(feats.reshape(-1, 8, fc), axis=0)
        part = sum(part[:, i * 128 : (i + 1) * 128] for i in range(fc // 128))
        tot = part if tot is None else tot + part
    p_ref[...] = acc.astype(p_ref.dtype)

    @pl.when(pl.program_id(0) == 0)
    def _():
        sp_ref[...] = jnp.zeros_like(sp_ref)

    sp_ref[...] += tot


def encode(c, enc, bias, dec, tm=384, fc=512):
    t, d = c.shape
    nf = enc.shape[1]
    return pl.pallas_call(
        functools.partial(encode_body, fc),
        grid=(t // tm,),
        in_specs=[
            pl.BlockSpec((tm, d), lambda i: (i, 0)),
            pl.BlockSpec((d, nf), lambda i: (0, 0)),
            pl.BlockSpec((1, nf), lambda i: (0, 0)),
            pl.BlockSpec((nf, d), lambda i: (0, 0)),
        ],
        out_specs=[
            pl.BlockSpec((tm, nf), lambda i: (i, 0)),
            pl.BlockSpec((tm, nf), lambda i: (i, 0)),
            pl.BlockSpec((tm, d), lambda i: (i, 0)),
            pl.BlockSpec((8, 128), lambda i: (0, 0)),
        ],
        out_shape=[
            jax.ShapeDtypeStruct((t, nf), BF),
            jax.ShapeDtypeStruct((t, nf), BF),
            jax.ShapeDtypeStruct((t, d), BF),
            jax.ShapeDtypeStruct((8, 128), F32),
        ],
        compiler_params=params(),
        cost_estimate=pl.CostEstimate(
            flops=4 * t * d * nf, bytes_accessed=4 * d * nf + 4 * t * nf + 4 * t * d, transcendentals=3 * t * nf
        ),
    )(c, enc, bias, dec)


def grad_dec_body(n, has, *refs):
    feats, grads, rest = refs[:n], refs[n : 2 * n], refs[2 * n :]
    acc = rest[0][...] if has else None
    out = rest[-1]
    for f, g in zip(feats, grads):
        d = lax.dot_general(f[...], g[...], TN, preferred_element_type=F32)
        acc = d if acc is None else acc + d
    out[...] = acc.astype(out.dtype)


def grad_dec(feats, grads, acc, dtype, fb=512):
    n, nf, d = len(feats), feats[0].shape[1], grads[0].shape[1]
    t = sum(f.shape[0] for f in feats)
    has = acc is not None
    block = pl.BlockSpec((fb, d), lambda i: (i, 0))
    return pl.pallas_call(
        functools.partial(grad_dec_body, n, has),
        grid=(nf // fb,),
        in_specs=[pl.BlockSpec((f.shape[0], fb), lambda i: (0, i)) for f in feats]
        + [pl.BlockSpec(g.shape, lambda i: (0, 0)) for g in grads]
        + [block] * has,
        out_specs=block,
        out_shape=jax.ShapeDtypeStruct((nf, d), dtype),
        compiler_params=params(),
        cost_estimate=pl.CostEstimate(
            flops=2 * t * d * nf, bytes_accessed=2 * t * (d + nf) + 4 * nf * d * (1 + has), transcendentals=0
        ),
    )(*feats, *grads, *([acc] * has))


def grad_enc_body(n, has, *refs):
    sigs, grads, cents, dec, rest = refs[:n], refs[n : 2 * n], refs[2 * n : 3 * n], refs[3 * n], refs[3 * n + 1 :]
    acc = rest[0][...] if has else None
    tot = rest[1][...] if has else None
    out, out_tot = rest[-2:]
    for s, g, c in zip(sigs, grads, cents):
        gf = lax.dot_general(g[...], dec[...], NT, preferred_element_type=F32)
        gp = (gf + sparsity_cost) * s[...].astype(F32)
        part = jnp.sum(gp, axis=0, keepdims=True)
        tot = part if tot is None else tot + part
        d = lax.dot_general(c[...], gp.astype(BF), TN, preferred_element_type=F32)
        acc = d if acc is None else acc + d
    out[...] = acc.astype(out.dtype)
    out_tot[...] = tot


def grad_enc(sigs, grads, cents, dec, acc, tot, dtype, fb=512):
    n = len(sigs)
    nf, d = dec.shape
    t = sum(s.shape[0] for s in sigs)
    has = acc is not None
    out_specs = [pl.BlockSpec((d, fb), lambda i: (0, i)), pl.BlockSpec((1, fb), lambda i: (0, i))]
    return pl.pallas_call(
        functools.partial(grad_enc_body, n, has),
        grid=(nf // fb,),
        in_specs=[pl.BlockSpec((s.shape[0], fb), lambda i: (0, i)) for s in sigs]
        + [pl.BlockSpec(g.shape, lambda i: (0, 0)) for g in grads]
        + [pl.BlockSpec(c.shape, lambda i: (0, 0)) for c in cents]
        + [pl.BlockSpec((fb, d), lambda i: (i, 0))]
        + out_specs * has,
        out_specs=out_specs,
        out_shape=[jax.ShapeDtypeStruct((d, nf), dtype), jax.ShapeDtypeStruct((1, nf), F32)],
        compiler_params=params(),
        cost_estimate=pl.CostEstimate(
            flops=4 * t * d * nf, bytes_accessed=2 * t * (2 * d + nf) + 4 * nf * d * (1 + has), transcendentals=0
        ),
    )(*sigs, *grads, *cents, dec, *([acc, tot] if has else []))


def depth_sum(g, z):
    q = g.shape[0] // 4

    def take(k):
        return lax.dynamic_slice_in_dim(g, lax.rem(z + k, 4) * q, q, 0)

    far = take(2)
    total = ring_scatter(take(0), take(3), take(1), far[: q // 2], far[q // 2 :], DEPTH).astype(BF)
    p, m, top, bottom = ring_gather(total, DEPTH)
    out = jnp.zeros_like(g)
    for k, v in ((0, total), (3, p), (1, m), (2, jnp.concatenate([top, bottom], 0))):
        out = lax.dynamic_update_slice_in_dim(out, v, lax.rem(z + k, 4) * q, 0)
    return out.astype(F32)


def advance(master, moment, average, grad, rate, rows_unit):
    moment_new = momentum_rate * moment + grad
    master_new = master - rate * (grad + momentum_rate * moment_new)
    if rows_unit:
        master_new = master_new * lax.rsqrt(jnp.sum(master_new * master_new, axis=1, keepdims=True) + 1e-06)
    return (master_new, moment_new, average_rate * average + (1.0 - average_rate) * master_new)


def on_device(
    acts,
    valid,
    enc_master,
    enc_bias,
    dec_master,
    dec_bias,
    enc_moment,
    enc_bias_moment,
    dec_moment,
    dec_bias_moment,
    enc_average,
    enc_bias_average,
    dec_average,
    dec_bias_average,
):
    width = acts.shape[1]
    heads = width // HEAD
    z = lax.axis_index("dp")
    weight = 0.5 + (jnp.arange(width) // HEAD).astype(F32) / (heads - 1)
    flags = valid.astype(F32)
    acts_f = acts.astype(F32)
    centered = jnp.where(valid[:, None] > 0, acts_f - dec_bias, SENTINEL).astype(BF)

    enc_low = enc_master.astype(BF)
    dec_low = dec_master.astype(BF)
    enc_two = jnp.concatenate([enc_low, swap(enc_low, 1)], 1)
    dec_two = jnp.concatenate([dec_low, swap(dec_low, 1)], 0)
    bias_two = jnp.concatenate([enc_bias, swap(enc_bias, 1)], 0)[None, :]

    def spread(block):
        p, m, top, bottom = ring_gather(block, INNER)
        mine = jnp.concatenate([block, p, m, top, bottom], 0)
        return (mine,) + ring_gather(mine, OUTER)

    groups = spread(centered)
    coded = [encode(g, enc_two, bias_two, dec_two) for g in groups]
    feats = [c[0] for c in coded]
    sigs = [c[1] for c in coded]
    parts = [c[2] for c in coded]
    sparse = sparsity_cost * sum(jnp.sum(c[3]) for c in coded)

    mine = ring_scatter(*parts, OUTER)
    q = acts.shape[0]
    decoded = ring_scatter(
        mine[:q], mine[q : 2 * q], mine[2 * q : 3 * q], mine[3 * q : 3 * q + q // 2], mine[3 * q + q // 2 :], INNER
    )

    err = decoded + dec_bias - acts_f
    direct = 2.0 * flags[:, None] * weight * err
    square = jnp.sum(flags[:, None] * weight * err * err)
    bias_direct = jnp.sum(direct, axis=0)

    grads = spread(direct.astype(BF))
    g_dec = grad_dec(feats[:3], grads[:3], None, F32)
    g_enc, g_sum = grad_enc(sigs[:3], grads[:3], groups[:3], dec_two, None, None, F32)
    g_dec = grad_dec(feats[3:], grads[3:], g_dec, BF)
    g_enc, g_sum = grad_enc(sigs[3:], grads[3:], groups[3:], dec_two, g_enc, g_sum, BF)

    n = enc_low.shape[1]
    g_dec = (g_dec[:n].astype(F32) + swap(g_dec[n:], 1).astype(F32)).astype(BF)
    g_enc = (g_enc[:, :n].astype(F32) + swap(g_enc[:, n:], 1).astype(F32)).astype(BF)
    g_dec = depth_sum(g_dec, z)
    g_enc = depth_sum(g_enc, z)

    through = jnp.sum(enc_two.astype(F32) * g_sum, axis=1)
    few = jnp.concatenate([bias_direct - through, jnp.stack([square + sparse, jnp.sum(flags)]), jnp.zeros((254,), F32)])
    got = swap(jnp.concatenate([few, g_sum[0, n:]]), 1)
    both = jnp.concatenate([few, g_sum[0, :n]]) + got
    for bit in (32, 64):
        both = both + swap(both, bit)
    few, g_enc_bias = both[:1024], both[1024:]
    for bit in (2, 4, 8, 16):
        few = few + swap(few, bit)
    loss_sum, count = few[width], few[width + 1]
    scale = 1.0 / count
    g_dec_bias = few[:width] * scale

    enc_new, enc_moment_new, enc_average_new = advance(enc_master, enc_moment, enc_average, g_enc * scale, 0.3, False)
    enc_bias_new, enc_bias_moment_new, enc_bias_average_new = advance(
        enc_bias, enc_bias_moment, enc_bias_average, g_enc_bias * scale, 2.0, False
    )
    dec_new, dec_moment_new, dec_average_new = advance(dec_master, dec_moment, dec_average, g_dec * scale, 0.3, True)
    dec_bias_new, dec_bias_moment_new, dec_bias_average_new = advance(
        dec_bias, dec_bias_moment, dec_bias_average, g_dec_bias, 0.1, False
    )
    return (
        loss_sum,
        count,
        enc_new,
        enc_bias_new,
        dec_new,
        dec_bias_new,
        enc_moment_new,
        enc_bias_moment_new,
        dec_moment_new,
        dec_bias_moment_new,
        enc_average_new,
        enc_bias_average_new,
        dec_average_new,
        dec_bias_average_new,
    )


def solution(mesh):
    placed = (
        P(("dp", "feat"), None),
        P(("dp", "feat")),
        P(None, "feat"),
        P("feat"),
        P("feat", None),
        P(),
        P(None, "feat"),
        P("feat"),
        P("feat", None),
        P(),
        P(None, "feat"),
        P("feat"),
        P("feat", None),
        P(),
    )
    return jax.shard_map(
        on_device,
        mesh=mesh,
        in_specs=placed,
        out_specs=(
            P(),
            P(),
            P(None, "feat"),
            P("feat"),
            P("feat", None),
            P(),
            P(None, "feat"),
            P("feat"),
            P("feat", None),
            P(),
            P(None, "feat"),
            P("feat"),
            P("feat", None),
            P(),
        ),
        check_vma=False,
    )
```

```python
import functools
import itertools

import jax
import jax.numpy as jnp
from jax import lax
from jax.experimental import pallas as pl
from jax.experimental.pallas import tpu as pltpu
from jax.sharding import PartitionSpec as P

HEAD = 64
F32 = jnp.float32
BF = jnp.bfloat16

sparsity_cost = 0.2
momentum_rate = 0.9
average_rate = 0.8

AXES = ("dp", "feat")
DEPTH = ("z", "z")
SENTINEL = 1000.0
TN = (((0,), (0,)), ((), ()))
NT = (((1,), (1,)), ((), ()))
COST = pl.CostEstimate(flops=10**6, bytes_accessed=10**3, transcendentals=0)


def step_pairs(first, second, shift):
    pairs = []
    for z, y, x, c in itertools.product(range(4), range(4), range(4), range(2)):
        at = {"z": z, "y": y, "x": x}
        axis = first if c == 0 else second
        to = dict(at)
        to[axis] = (at[axis] + shift) % 4
        pairs.append((((z * 4 + y) * 4 + x) * 2 + c, ((to["z"] * 4 + to["y"]) * 4 + to["x"]) * 2 + c))
    return pairs


def move(v, axes, shift):
    return lax.ppermute(v, AXES, step_pairs(axes[0], axes[1], shift))


def swap(v, bit):
    return lax.ppermute(v, AXES, [(i, i ^ bit) for i in range(128)])


INNER = ("x", "y")
OUTER = ("y", "x")
NEAR = ((1, 3), (3, 1))


def trade(v, which):
    pairs = []
    for i in range(128):
        z, rest = divmod(i, 32)
        pairs.append((i, (z ^ NEAR[rest % 2][which]) * 32 + rest))
    return lax.ppermute(v, AXES, pairs)


def after(x, *deps):
    return lax.optimization_barrier((x,) + deps)[0]


def direct_gather(block, axes):
    return move(block, axes, 1), move(block, axes, 3), move(block, axes, 2)


def direct_scatter(p, m, far, axes):
    return move(p, axes, 3), move(m, axes, 1), move(far, axes, 2)


def ring_gather(block, axes, between=None):
    half = block.shape[0] // 2
    p = move(block, axes, 1)
    m = move(block, axes, 3)
    if between is not None:
        p, m = between(p, m)
    return p, m, move(p[:half], axes, 1), move(m[half:], axes, 3)


def ring_total(v, axes, *deps):
    p, m, far = direct_gather(v, axes)
    if deps:
        p, m, far = after((p, m, far), *deps)
    return (v + far) + (p + m)


def local(body, outs, args, scalars=(), aliases=None, mib=4):
    vmem = pl.BlockSpec(memory_space=pltpu.VMEM)
    return pl.pallas_call(
        body,
        in_specs=[pl.BlockSpec(memory_space=pltpu.SMEM)] * len(scalars) + [vmem] * len(args),
        out_specs=[vmem] * len(outs),
        out_shape=[pltpu.VMEM(shape, dtype) for shape, dtype in outs],
        input_output_aliases=aliases or {},
        compiler_params=pltpu.CompilerParams(vmem_limit_bytes=mib * 2**20),
        cost_estimate=COST,
    )(*scalars, *[pltpu.with_memory_space_constraint(v, pltpu.VMEM) for v in args])


def center_body(a_hbm, v_hbm, b_hbm, c_ref, a_ref, v_ref, b_ref, sems):
    pairs = ((a_hbm, a_ref), (v_hbm, v_ref), (b_hbm, b_ref))
    copies = [pltpu.make_async_copy(s, d, sems.at[i]) for i, (s, d) in enumerate(pairs)]
    for copy in copies:
        copy.start()
    for copy in copies:
        copy.wait()
    n = a_ref.shape[0]
    same = lax.broadcasted_iota(jnp.int32, (n, n), 0) == lax.broadcasted_iota(jnp.int32, (n, n), 1)
    flag = jnp.sum(jnp.where(same, v_ref[...].astype(F32)[None, :], 0.0), axis=1, keepdims=True)
    c_ref[...] = jnp.where(flag > 0.5, a_ref[...].astype(F32) - b_ref[...][None, :], SENTINEL).astype(BF)


def center(acts, valid, bias):
    args = (acts, valid, bias)
    return pl.pallas_call(
        center_body,
        in_specs=[pl.BlockSpec(memory_space=pl.ANY)] * 3,
        out_specs=pl.BlockSpec(memory_space=pltpu.VMEM),
        out_shape=pltpu.VMEM(acts.shape, BF),
        scratch_shapes=[pltpu.VMEM(v.shape, v.dtype) for v in args] + [pltpu.SemaphoreType.DMA((3,))],
        compiler_params=pltpu.CompilerParams(vmem_limit_bytes=4 * 2**20),
        cost_estimate=COST,
    )(*[pltpu.with_memory_space_constraint(v, pltpu.HBM) for v in args])


def stack_body(*refs):
    at = 0
    for r in refs[:-1]:
        refs[-1][at : at + r.shape[0], :] = r[...]
        at += r.shape[0]


def stack(*arrays):
    rows = sum(v.shape[0] for v in arrays)
    return local(stack_body, [((rows, arrays[0].shape[1]), arrays[0].dtype)], arrays)[0]


def total_body(a_ref, b_ref, out_ref):
    out_ref[...] = (a_ref[...].astype(F32) + b_ref[...].astype(F32)).astype(BF)


def total_low(a, b):
    return local(total_body, [(a.shape, BF)], (a, b))[0]


def near_body(at, y_ref, p_ref, m_ref, out_ref):
    rows = slice(at, at + out_ref.shape[0])
    out_ref[...] = y_ref[rows, :].astype(F32) + (p_ref[...].astype(F32) + m_ref[...].astype(F32))


def near_sum(y, p, m, at):
    return local(functools.partial(near_body, at), [(p.shape, F32)], (y, p, m))[0]


def halves_body(s_ref, f_ref, *out_refs):
    q = out_refs[0].shape[0]
    for k, out in enumerate(out_refs):
        rows = slice(k * q, (k + 1) * q)
        out[...] = (s_ref[rows, :] + f_ref[rows, :].astype(F32)).astype(out.dtype)


def outer_sum(near, far, dtype):
    rows, d = far.shape
    return local(halves_body, [((rows // 2, d), dtype), ((rows // 2, d), BF)], (near, far))


def error_body(m_ref, p_ref, n_ref, f_ref, a_ref, v_ref, b_ref, l_ref, g_ref, few_ref):
    n, d = a_ref.shape
    same = lax.broadcasted_iota(jnp.int32, (n, n), 0) == lax.broadcasted_iota(jnp.int32, (n, n), 1)
    flag = jnp.sum(jnp.where(same, v_ref[...].astype(F32), 0.0), axis=1, keepdims=True)
    head = (lax.broadcasted_iota(jnp.int32, (1, d), 1) // HEAD).astype(F32)
    weight = 0.5 + head / (d // HEAD - 1)
    decoded = m_ref[...] + (p_ref[...].astype(F32) + n_ref[...].astype(F32) + f_ref[...].astype(F32))
    err = decoded + b_ref[...] - a_ref[...].astype(F32)
    part = flag * weight * err
    direct = 2.0 * part
    g_ref[...] = direct.astype(BF)
    few_ref[:, :d] = jnp.sum(direct, axis=0, keepdims=True)
    loss = jnp.sum(jnp.sum(part * err, axis=0, keepdims=True), axis=1, keepdims=True)
    loss += sparsity_cost * jnp.sum(jnp.sum(l_ref[...], axis=0, keepdims=True), axis=1, keepdims=True)
    lane = lax.broadcasted_iota(jnp.int32, (1, 128), 1)
    few_ref[:, d:] = jnp.where(lane == 0, loss, 0.0)


def through_body(few_ref, t_ref, u_ref, enc_ref, mine_ref, other_ref):
    n, d = t_ref.shape[1], enc_ref.shape[0]
    row = lax.broadcasted_iota(jnp.int32, (16, n), 0)
    moved = None
    for k, r in enumerate((t_ref, u_ref)):
        tot = r[...]
        high = tot.astype(BF).astype(F32)
        mid = (tot - high).astype(BF).astype(F32)
        low = tot - high - mid
        terms = jnp.where(row == 0, high, jnp.where(row == 1, mid, jnp.where(row == 2, low, 0.0))).astype(BF)
        v = lax.dot_general(terms, enc_ref[:, k * n : (k + 1) * n], NT, preferred_element_type=F32)
        v = jnp.sum(v, axis=0, keepdims=True)
        moved = v if moved is None else moved + v
    for out, r in ((mine_ref, t_ref), (other_ref, u_ref)):
        out[:, :d] = few_ref[:, :d] - moved
        out[:, d : d + 128] = few_ref[:, d:]
        out[:, d + 128 :] = r[...]


def small_sums(few, t_mine, t_other, enc):
    shape = (1, few.shape[1] + t_mine.shape[1])
    return local(through_body, [(shape, F32)] * 2, (few, t_mine, t_other, enc))


def activate(pre):
    t = jnp.exp2(jnp.abs(pre) * -1.4426950408889634)
    u = 1.0 + t
    log = jnp.where(t < 1e-3, t * (1.0 - 0.5 * t), jnp.log2(u) * 0.6931471805599453)
    r = pltpu.reciprocal(u, approx=True)
    return jnp.maximum(pre, 0.0) + log, jnp.where(pre >= 0, r, t * r)


def encode_body(n, tm, fc, *refs):
    parts = refs[:n]
    enc_ref, b_ref, dec_ref, f_ref, s_ref, l_ref, n_ref = refs[n : n + 7]
    tot = None
    counted = 0.0
    at = 0
    for c_ref, p_ref in zip(parts, refs[n + 7 :]):
        for i in range(c_ref.shape[0] // tm):
            rows = slice(at, at + tm)
            at += tm
            c = c_ref[i * tm : (i + 1) * tm, :]
            out = c[:, 0:1].astype(F32) > 0.5 * SENTINEL
            off = jnp.where(out, -1e30, 0.0)
            counted += jnp.sum(jnp.where(out, 0.0, 1.0), axis=0, keepdims=True)
            acc = None
            for k in range(enc_ref.shape[1] // fc):
                sl = slice(k * fc, (k + 1) * fc)
                pre = jnp.dot(c, enc_ref[:, sl], preferred_element_type=F32) + b_ref[:, sl] + off
                feats, sig = activate(pre)
                low = feats.astype(BF)
                f_ref[rows, sl] = low
                s_ref[rows, sl] = sig.astype(BF)
                d = jnp.dot(low, dec_ref[sl, :], preferred_element_type=F32)
                acc = d if acc is None else acc + d
                part = jnp.sum(feats.reshape(-1, 8, fc), axis=0)
                part = sum(part[:, j * 128 : (j + 1) * 128] for j in range(fc // 128))
                tot = part if tot is None else tot + part
            p_ref[i * tm : (i + 1) * tm, :] = acc.astype(p_ref.dtype)
    l_ref[...] = tot
    n_ref[...] = jnp.broadcast_to(counted, n_ref.shape)


def encode(parts, enc, bias, dec, tm=384, fc=768):
    t = sum(c.shape[0] for c in parts)
    d, nf = enc.shape
    outs = [((t, nf), BF), ((t, nf), BF), ((8, 128), F32), ((8, 128), F32)] + [(c.shape, BF) for c in parts]
    return local(functools.partial(encode_body, len(parts), tm, fc), outs, (*parts, enc, bias, dec))


def flatten(groups):
    arrays, spec = [], []
    for group in groups:
        spec.append([])
        for part in group:
            spec[-1].append([])
            for v, a, b in part:
                k = next((i for i, w in enumerate(arrays) if w is v), len(arrays))
                if k == len(arrays):
                    arrays.append(v)
                spec[-1][-1].append((k, a, b))
    return arrays, spec


def rows_of(refs, part, lanes=slice(None)):
    blocks = [refs[k][a:b, lanes] for k, a, b in part]
    return blocks[0] if len(blocks) == 1 else jnp.concatenate(blocks, 0)


def grad_dec_body(spec, n, has, start, fb, *refs):
    rest = refs[n:]
    out = rest[-1]
    for k in range(out.shape[0] // fb):
        sl = slice(start + k * fb, start + (k + 1) * fb)
        acc = rest[0][sl, :] if has else None
        for f, g in spec:
            d = lax.dot_general(rows_of(refs, f, sl), rows_of(refs, g), TN, preferred_element_type=F32)
            acc = d if acc is None else acc + d
        out[k * fb : (k + 1) * fb, :] = acc.astype(out.dtype)


def grad_dec(groups, acc, dtype, shape, start=0, size=None, fb=384):
    arrays, spec = flatten(groups)
    n = len(arrays)
    nf, d = shape
    size = nf if size is None else size
    has = acc is not None
    return local(
        functools.partial(grad_dec_body, spec, n, has, start, fb),
        [((size, d), dtype)],
        (*arrays, *([acc] * has)),
        aliases={n: 0} if has and dtype == F32 else {},
    )[0]


def grad_enc_body(spec, n, has, start, fb, *refs):
    dec, rest = refs[n], refs[n + 1 :]
    out, out_tot = rest[-2:]
    for k in range(out.shape[1] // fb):
        sl = slice(start + k * fb, start + (k + 1) * fb)
        ol = slice(k * fb, (k + 1) * fb)
        acc = rest[0][:, sl] if has else None
        tot = rest[1][:, sl] if has else None
        for s, g, c in spec:
            gf = lax.dot_general(rows_of(refs, g), dec[sl, :], NT, preferred_element_type=F32)
            gp = (gf + sparsity_cost) * rows_of(refs, s, sl).astype(F32)
            part = jnp.sum(gp, axis=0, keepdims=True)
            tot = part if tot is None else tot + part
            d = lax.dot_general(rows_of(refs, c), gp.astype(BF), TN, preferred_element_type=F32)
            acc = d if acc is None else acc + d
        out[:, ol] = acc.astype(out.dtype)
        out_tot[:, ol] = tot


def grad_enc(groups, dec, acc, tot, dtype, start=0, size=None, fb=384):
    arrays, spec = flatten(groups)
    n = len(arrays)
    nf, d = dec.shape
    size = nf if size is None else size
    has = acc is not None
    outs = [((d, size), dtype), ((1, size), F32)]
    aliases = {n + 1: 0, n + 2: 1} if has and dtype == F32 else {}
    args = (*arrays, dec, *([acc, tot] if has else []))
    return local(functools.partial(grad_enc_body, spec, n, has, start, fb), outs, args, aliases=aliases)


def split_body(bit_ref, *refs):
    send, keep = refs[-2:]
    rows = keep.shape[0]
    here = pl.multiple_of(bit_ref[0] * rows, rows)
    there = pl.multiple_of((1 - bit_ref[0]) * rows, rows)
    send[...] = sum(r[pl.ds(there, rows), :].astype(F32) for r in refs[:-2]).astype(BF)
    keep[...] = sum(r[pl.ds(here, rows), :].astype(F32) for r in refs[:-2])


def split_sum(arrays, bit):
    rows, d = arrays[0].shape
    return local(split_body, [((rows // 2, d), BF), ((rows // 2, d), F32)], arrays, (bit,))


def update_body(rate, rows_unit, order_ref, n_ref, g_ref, w_ref, m_ref, a_ref, *refs):
    w_out, m_out, a_out = refs[-3:]
    g = g_ref[...].astype(F32) * (1.0 / n_ref[:1, :1])
    w_out[...], m_out[...], a_out[...] = advance(w_ref[...], m_ref[...], a_ref[...], g, rate, rows_unit)


def update(g, order, count, weights, rate, rows_unit, made=None):
    q = g.shape[0] // 2
    d = g.shape[1]
    there = pl.BlockSpec((q, d), lambda i, order: (order[i], 0))
    return pl.pallas_call(
        functools.partial(update_body, rate, rows_unit),
        grid_spec=pltpu.PrefetchScalarGridSpec(
            num_scalar_prefetch=1,
            grid=(2,),
            in_specs=[
                pl.BlockSpec((8, 128), lambda i, order: (0, 0)),
                pl.BlockSpec((q, d), lambda i, order: (i, 0)),
                there,
                there,
                there,
            ]
            + ([pl.BlockSpec(memory_space=pl.ANY)] * 3 if made else []),
            out_specs=[there] * 3,
        ),
        out_shape=[jax.ShapeDtypeStruct(weights[0].shape, F32)] * 3,
        input_output_aliases={6: 0, 7: 1, 8: 2} if made else {},
        compiler_params=pltpu.CompilerParams(dimension_semantics=("arbitrary",), vmem_limit_bytes=14 * 2**20),
        cost_estimate=COST,
    )(
        order,
        count,
        pltpu.with_memory_space_constraint(g, pltpu.VMEM),
        *weights,
        *(made or []),
    )


def advance(master, moment, average, grad, rate, rows_unit):
    moment_new = momentum_rate * moment + grad
    master_new = master - rate * (grad + momentum_rate * moment_new)
    if rows_unit:
        master_new = master_new * lax.rsqrt(jnp.sum(master_new * master_new, axis=1, keepdims=True) + 1e-06)
    return (master_new, moment_new, average_rate * average + (1.0 - average_rate) * master_new)


def on_device(
    acts,
    valid,
    enc_master,
    enc_bias,
    dec_master,
    dec_bias,
    enc_moment,
    enc_bias_moment,
    dec_moment,
    dec_bias_moment,
    enc_average,
    enc_bias_average,
    dec_average,
    dec_bias_average,
):
    q, width = acts.shape
    heads = width // HEAD
    z = lax.axis_index("dp")
    core = lax.rem(lax.axis_index("feat"), 2)
    high = z // 2
    mixed = lax.rem(z + high, 2)
    bit_1 = jnp.where(core == 0, mixed, high)
    bit_2 = jnp.where(core == 0, high, mixed)
    bit_1 = bit_1.astype(jnp.int32)[None]
    bit_2 = bit_2.astype(jnp.int32)[None]
    valid_row = valid[None]
    bias_row = dec_bias[None]
    order_1 = jnp.concatenate([bit_1 * 2 + bit_2, bit_1 * 2 + 1 - bit_2])
    order_2 = jnp.concatenate([(1 - bit_1) * 2 + bit_2, (1 - bit_1) * 2 + 1 - bit_2])
    acts = after(acts, bit_1, bit_2, order_1, order_2)
    centered = center(acts, valid, dec_bias)

    near = direct_gather(centered, INNER)
    n = enc_master.shape[1]
    both = jnp.concatenate([enc_master.astype(BF), dec_master.astype(BF)], 0)
    other = swap(after(both, *near), 1)
    bias_two = jnp.concatenate([enc_bias, swap(after(enc_bias, *near), 1)], 0)[None, :]

    c_own = stack(centered, *near)
    enc_two = jnp.concatenate([both[:width], other[:width]], 1)
    dec_two = jnp.concatenate([both[width:], other[width:]], 0)
    h = 2 * q
    f_own, s_own, l_own, n_own, y_own = encode([c_own], enc_two, bias_two, dec_two)
    c_p, c_m, c_top, c_bottom = ring_gather(c_own, OUTER, lambda p, m: after((p, m), n_own))
    f_t, s_t, l_t, n_t, y_pt, y_mt = encode([c_p[:h], c_m[:h]], enc_two, bias_two, dec_two)
    rest = after([c_p[h:], c_m[h:]], n_t)
    f_b, s_b, l_b, n_b, y_pb, y_mb = encode(rest, enc_two, bias_two, dec_two)
    c_top, c_bottom = after((c_top, c_bottom), n_b)
    f_fb, s_fb, l_fb, n_fb, y_fb = encode([c_bottom], enc_two, bias_two, dec_two)
    near_t = near_sum(y_own, move(y_pt, OUTER, 3), move(y_mt, OUTER, 1), 0)
    f_ft, s_ft, l_ft, n_ft, y_ft = encode([after(c_top, n_fb, near_t)], enc_two, bias_two, dec_two)
    near_b = near_sum(y_own, move(y_pb, OUTER, 3), move(y_mb, OUTER, 1), h)
    far_b = move(y_fb, OUTER, 2)
    far_t = move(y_ft, OUTER, 2)

    count = n_own + n_t + n_b + n_fb + n_ft
    sparse = l_own + l_t + l_b + l_fb + l_ft
    count = count + swap(after(count, near_b, near_t), 1)

    to_m, to_far = outer_sum(near_b, far_b, BF)
    mine, to_p = outer_sum(near_t, after(far_t, sparse), F32)
    got = after(direct_scatter(to_p, to_m, to_far, INNER), count)
    g_block, few = local(
        error_body,
        [((q, width), BF), ((1, width + 128), F32)],
        (mine, *got, acts, valid_row, bias_row, sparse),
    )
    g_own = stack(g_block, *direct_gather(g_block, INNER))

    def all_rows(v):
        return [(v, 0, v.shape[0])]

    shape = dec_two.shape
    d_sum = grad_dec([(all_rows(f_own), all_rows(g_own))], None, F32, shape)
    e_sum, e_tot = grad_enc([(all_rows(s_own), all_rows(g_own), all_rows(c_own))], dec_two, None, None, F32)
    count = ring_total(after(count, e_tot), DEPTH)
    g_p, g_m, g_top, g_bottom = ring_gather(g_own, OUTER, lambda p, m: after((p, m), e_tot, d_sum, count))
    from_p = [(s_t, 0, h), (s_b, 0, h)], all_rows(g_p), all_rows(c_p)
    from_m = [(s_t, h, 2 * h), (s_b, h, 2 * h)], all_rows(g_m), all_rows(c_m)
    e_sum, e_tot = grad_enc([from_p, from_m], dec_two, e_sum, e_tot, F32)
    g_top, g_bottom = after([g_top, g_bottom], e_tot)

    def far(top, bottom):
        return all_rows(top) + all_rows(bottom)

    e_far = [(far(s_ft, s_fb), far(g_top, g_bottom), far(c_top, c_bottom))]
    e_other, t_other = grad_enc(e_far, dec_two, e_sum, e_tot, BF, n, n)
    e_got = swap(e_other, 1)
    g_top, g_bottom = after([g_top, g_bottom], t_other)
    e_far = [(far(s_ft, s_fb), far(g_top, g_bottom), far(c_top, c_bottom))]
    e_mine, t_mine = grad_enc(e_far, dec_two, e_sum, e_tot, BF, 0, n)
    e_send, e_keep = split_sum([e_mine, e_got], bit_1)

    def d_groups(after_what):
        a, b, c, d = after([g_p, g_m, g_top, g_bottom], after_what)
        return [
            ([(f_t, 0, h), (f_b, 0, h)], all_rows(a)),
            ([(f_t, h, 2 * h), (f_b, h, 2 * h)], all_rows(b)),
            (far(f_ft, f_fb), far(c, d)),
        ]

    d_other = grad_dec(d_groups(e_keep), d_sum, BF, shape, n, n)
    d_got = swap(d_other, 1)
    d_mine = grad_dec(d_groups(d_other), d_sum, BF, shape, 0, n)
    few_mine, few_other = small_sums(after(few, d_mine), t_mine, t_other, enc_two)
    d_send, d_keep = split_sum([d_mine, d_got], bit_1)

    e_send, e_keep = split_sum([e_keep, after(trade(e_send, 0), d_send, few_mine)], bit_2)
    few = few_mine + after(swap(few_other, 1), e_send)
    few, g_enc_bias = few[:, : width + 128], few[:, width + 128 :]
    d_send, d_keep = split_sum([d_keep, after(trade(d_send, 0), few)], bit_2)
    few = few + after(swap(few, 2), d_send)
    e_total = total_low(e_keep, after(trade(e_send, 1), few))
    few = few + after(swap(few, 6), e_total)
    d_total = total_low(d_keep, after(trade(d_send, 1), few))
    few = few + after(swap(few, 8), d_total)
    e_half = stack(e_total, after(trade(e_total, 1), few))
    few = few + after(swap(few, 24), e_half)
    few = jnp.concatenate([few, g_enc_bias], 1)
    d_half = stack(d_total, after(trade(d_total, 1), few))
    e_half = after(e_half, d_half), trade(e_half, 0)
    d_half = d_half, trade(d_half, 0)
    enc_weights = enc_master, enc_moment, enc_average
    dec_weights = dec_master, dec_moment, dec_average
    enc_made = update(e_half[0], order_1, count, enc_weights, 0.3, False)
    few = few + after(swap(few, 32), enc_made[0])
    enc_new, enc_moment_new, enc_average_new = update(
        after(e_half[1], few), order_2, count, enc_weights, 0.3, False, enc_made
    )
    dec_made = update(after(d_half[0], enc_new), order_1, count, dec_weights, 0.3, True)
    few = few + after(swap(few, 96), dec_made[0])
    scale = 1.0 / count[:1, :1]
    loss_sum = few[0, width]
    g_enc_bias = few[0, width + 128 :] * scale[0]
    g_dec_bias = few[0, :width] * scale[0]
    enc_bias_new, enc_bias_moment_new, enc_bias_average_new = advance(
        enc_bias, enc_bias_moment, enc_bias_average, g_enc_bias, 2.0, False
    )
    dec_bias_new, dec_bias_moment_new, dec_bias_average_new = advance(
        dec_bias, dec_bias_moment, dec_bias_average, g_dec_bias, 0.1, False
    )
    dec_new, dec_moment_new, dec_average_new = update(
        after(d_half[1], enc_bias_new, dec_bias_new), order_2, count, dec_weights, 0.3, True, dec_made
    )
    count = count[0, 0]
    return (
        loss_sum,
        count,
        enc_new,
        enc_bias_new,
        dec_new,
        dec_bias_new,
        enc_moment_new,
        enc_bias_moment_new,
        dec_moment_new,
        dec_bias_moment_new,
        enc_average_new,
        enc_bias_average_new,
        dec_average_new,
        dec_bias_average_new,
    )


def solution(mesh):
    placed = (
        P(("dp", "feat"), None),
        P(("dp", "feat")),
        P(None, "feat"),
        P("feat"),
        P("feat", None),
        P(),
        P(None, "feat"),
        P("feat"),
        P("feat", None),
        P(),
        P(None, "feat"),
        P("feat"),
        P("feat", None),
        P(),
    )
    return jax.shard_map(
        on_device,
        mesh=mesh,
        in_specs=placed,
        out_specs=(
            P(),
            P(),
            P(None, "feat"),
            P("feat"),
            P("feat", None),
            P(),
            P(None, "feat"),
            P("feat"),
            P("feat", None),
            P(),
            P(None, "feat"),
            P("feat"),
            P("feat", None),
            P(),
        ),
        check_vma=False,
    )
```

```python
import functools
import itertools

import jax
import jax.numpy as jnp
from jax import lax
from jax.experimental import pallas as pl
from jax.experimental.pallas import tpu as pltpu
from jax.sharding import PartitionSpec as P

HEAD = 64
F32 = jnp.float32
BF = jnp.bfloat16

sparsity_cost = 0.2
momentum_rate = 0.9
average_rate = 0.8

AXES = ("dp", "feat")
DEPTH = ("z", "z")
SENTINEL = 1000.0
TN = (((0,), (0,)), ((), ()))
NT = (((1,), (1,)), ((), ()))
COST = pl.CostEstimate(flops=10**6, bytes_accessed=10**3, transcendentals=0)


def step_pairs(first, second, shift):
    pairs = []
    for z, y, x, c in itertools.product(range(4), range(4), range(4), range(2)):
        at = {"z": z, "y": y, "x": x}
        axis = first if c == 0 else second
        to = dict(at)
        to[axis] = (at[axis] + shift) % 4
        pairs.append((((z * 4 + y) * 4 + x) * 2 + c, ((to["z"] * 4 + to["y"]) * 4 + to["x"]) * 2 + c))
    return pairs


def move(v, axes, shift):
    return lax.ppermute(v, AXES, step_pairs(axes[0], axes[1], shift))


def swap(v, bit):
    return lax.ppermute(v, AXES, [(i, i ^ bit) for i in range(128)])


INNER = ("x", "y")
OUTER = ("y", "x")
NEAR = ((1, 3), (3, 1))


def trade(v, which):
    pairs = []
    for i in range(128):
        z, rest = divmod(i, 32)
        pairs.append((i, (z ^ NEAR[rest % 2][which]) * 32 + rest))
    return lax.ppermute(v, AXES, pairs)


def after(x, *deps):
    return lax.optimization_barrier((x,) + deps)[0]


def direct_gather(block, axes):
    return move(block, axes, 1), move(block, axes, 3), move(block, axes, 2)


def direct_scatter(p, m, far, axes):
    return move(p, axes, 3), move(m, axes, 1), move(far, axes, 2)


def spread(block, between, early):
    q = block.shape[0]
    p, m, far = direct_gather(block, INNER)
    if not early:
        own = stack(block, p, m, far)
        p, m = move(own, OUTER, 1), move(own, OUTER, 3)
        p, m = after((p, m), *between(own))
        return own, [p], [m], move(p[: 2 * q], OUTER, 1), move(m[2 * q :], OUTER, 3)
    first = stack(block, p, m)
    p_1, m_1 = move(first, OUTER, 1), move(first, OUTER, 3)
    own = stack(first, far)
    p_2, m_2 = move(far, OUTER, 1), move(far, OUTER, 3)
    p_1, m_1 = after((p_1, m_1), *between(own))
    top_rows = p_1[: 2 * q]
    top = move(top_rows, OUTER, 1)
    p_2, m_2 = after((p_2, m_2), top_rows)
    bottom = move(stack((m_1, 2 * q, 3 * q), m_2), OUTER, 3)
    return own, [p_1, p_2], [m_1, m_2], top, bottom


def ring_total(v, axes, *deps):
    p, m, far = direct_gather(v, axes)
    if deps:
        p, m, far = after((p, m, far), *deps)
    return (v + far) + (p + m)


def local(body, outs, args, scalars=(), aliases=None, mib=4):
    vmem = pl.BlockSpec(memory_space=pltpu.VMEM)
    return pl.pallas_call(
        body,
        in_specs=[pl.BlockSpec(memory_space=pltpu.SMEM)] * len(scalars) + [vmem] * len(args),
        out_specs=[vmem] * len(outs),
        out_shape=[pltpu.VMEM(shape, dtype) for shape, dtype in outs],
        input_output_aliases=aliases or {},
        compiler_params=pltpu.CompilerParams(vmem_limit_bytes=mib * 2**20),
        cost_estimate=COST,
    )(*scalars, *[pltpu.with_memory_space_constraint(v, pltpu.VMEM) for v in args])


def center_body(a_hbm, v_hbm, b_hbm, c_ref, a_ref, v_ref, b_ref, sems):
    pairs = ((a_hbm, a_ref), (v_hbm, v_ref), (b_hbm, b_ref))
    copies = [pltpu.make_async_copy(s, d, sems.at[i]) for i, (s, d) in enumerate(pairs)]
    for copy in copies:
        copy.start()
    for copy in copies:
        copy.wait()
    n = a_ref.shape[0]
    same = lax.broadcasted_iota(jnp.int32, (n, n), 0) == lax.broadcasted_iota(jnp.int32, (n, n), 1)
    flag = jnp.sum(jnp.where(same, v_ref[...].astype(F32)[None, :], 0.0), axis=1, keepdims=True)
    c_ref[...] = jnp.where(flag > 0.5, a_ref[...].astype(F32) - b_ref[...][None, :], SENTINEL).astype(BF)


def center(acts, valid, bias):
    args = (acts, valid, bias)
    return pl.pallas_call(
        center_body,
        in_specs=[pl.BlockSpec(memory_space=pl.ANY)] * 3,
        out_specs=pl.BlockSpec(memory_space=pltpu.VMEM),
        out_shape=pltpu.VMEM(acts.shape, BF),
        scratch_shapes=[pltpu.VMEM(v.shape, v.dtype) for v in args] + [pltpu.SemaphoreType.DMA((3,))],
        compiler_params=pltpu.CompilerParams(vmem_limit_bytes=4 * 2**20),
        cost_estimate=COST,
    )(*[pltpu.with_memory_space_constraint(v, pltpu.HBM) for v in args])


def stack_body(ranges, *refs):
    at = 0
    for r, (a, b) in zip(refs, ranges):
        refs[-1][at : at + b - a, :] = r[a:b, :]
        at += b - a


def stack(*arrays):
    parts = [v if isinstance(v, tuple) else (v, 0, v.shape[0]) for v in arrays]
    ranges = [(a, b) for _, a, b in parts]
    arrays = [v for v, _, _ in parts]
    shape = (sum(b - a for a, b in ranges), arrays[0].shape[1])
    return local(functools.partial(stack_body, ranges), [(shape, arrays[0].dtype)], arrays)[0]


def total_body(a_ref, b_ref, out_ref):
    out_ref[...] = (a_ref[...].astype(F32) + b_ref[...].astype(F32)).astype(BF)


def total_low(a, b):
    return local(total_body, [(a.shape, BF)], (a, b))[0]


def near_body(at, y_ref, p_ref, m_ref, out_ref):
    rows = slice(at, at + out_ref.shape[0])
    out_ref[...] = y_ref[rows, :].astype(F32) + (p_ref[...].astype(F32) + m_ref[...].astype(F32))


def near_sum(y, p, m, at):
    return local(functools.partial(near_body, at), [(p.shape, F32)], (y, p, m))[0]


def halves_body(s_ref, f_ref, *out_refs):
    q = out_refs[0].shape[0]
    for k, out in enumerate(out_refs):
        rows = slice(k * q, (k + 1) * q)
        out[...] = (s_ref[rows, :] + f_ref[rows, :].astype(F32)).astype(out.dtype)


def outer_sum(near, far, dtype):
    rows, d = far.shape
    return local(halves_body, [((rows // 2, d), dtype), ((rows // 2, d), BF)], (near, far))


def error_body(m_ref, p_ref, n_ref, f_ref, a_ref, v_ref, b_ref, l_ref, g_ref, few_ref):
    n, d = a_ref.shape
    same = lax.broadcasted_iota(jnp.int32, (n, n), 0) == lax.broadcasted_iota(jnp.int32, (n, n), 1)
    flag = jnp.sum(jnp.where(same, v_ref[...].astype(F32), 0.0), axis=1, keepdims=True)
    head = (lax.broadcasted_iota(jnp.int32, (1, d), 1) // HEAD).astype(F32)
    weight = 0.5 + head / (d // HEAD - 1)
    decoded = m_ref[...] + (p_ref[...].astype(F32) + n_ref[...].astype(F32) + f_ref[...].astype(F32))
    err = decoded + b_ref[...] - a_ref[...].astype(F32)
    part = flag * weight * err
    direct = 2.0 * part
    g_ref[...] = direct.astype(BF)
    loss = jnp.sum(jnp.sum(part * err, axis=0, keepdims=True), axis=1, keepdims=True)
    loss += sparsity_cost * jnp.sum(jnp.sum(l_ref[...], axis=0, keepdims=True), axis=1, keepdims=True)
    row = lax.broadcasted_iota(jnp.int32, (8, d), 0)
    few_ref[...] = jnp.where(row == 0, jnp.sum(direct, axis=0, keepdims=True), jnp.where(row == 1, loss, 0.0))


def terms(v):
    high = v.astype(BF).astype(F32)
    mid = (v - high).astype(BF).astype(F32)
    return high, mid, v - high - mid


def pack(few):
    row = lax.broadcasted_iota(jnp.int32, (16, few.shape[1]), 0)
    out = jnp.zeros((16, few.shape[1]), F32)
    for k in range(3):
        for j, t in enumerate(terms(few[k : k + 1, :])):
            out = jnp.where(row == 3 * j + k, t, out)
    return out.astype(BF)


def unpack(packed):
    v = packed.astype(F32)
    row = lax.broadcasted_iota(jnp.int32, v.shape, 0)
    out_row = lax.broadcasted_iota(jnp.int32, (8, v.shape[1]), 0)
    out = jnp.zeros((8, v.shape[1]), F32)
    for k in range(3):
        mine = (row == k) | (row == k + 3) | (row == k + 6)
        out = jnp.where(out_row == k, jnp.sum(jnp.where(mine, v, 0.0), axis=0, keepdims=True), out)
    return out


def through_body(few_ref, t_ref, u_ref, enc_ref, mine_ref, other_ref):
    n = t_ref.shape[1]
    row = lax.broadcasted_iota(jnp.int32, (16, n), 0)
    moved = None
    for k, r in enumerate((t_ref, u_ref)):
        high, mid, low = terms(r[...])
        lhs = jnp.where(row == 0, high, jnp.where(row == 1, mid, jnp.where(row == 2, low, 0.0))).astype(BF)
        v = lax.dot_general(lhs, enc_ref[:, k * n : (k + 1) * n], NT, preferred_element_type=F32)
        v = jnp.sum(v, axis=0, keepdims=True)
        moved = v if moved is None else moved + v
    row = lax.broadcasted_iota(jnp.int32, few_ref.shape, 0)
    few = few_ref[...] - jnp.where(row == 0, moved, 0.0)
    mine_ref[...] = jnp.where(row == 2, t_ref[...], few)
    other_ref[...] = pack(jnp.where(row == 2, u_ref[...], few))


def small_sums(few, t_mine, t_other, enc):
    return local(through_body, [(few.shape, F32), ((16, few.shape[1]), BF)], (few, t_mine, t_other, enc))


def activate(pre):
    t = jnp.exp2(jnp.abs(pre) * -1.4426950408889634)
    u = 1.0 + t
    log = jnp.where(t < 1e-3, t * (1.0 - 0.5 * t), jnp.log2(u) * 0.6931471805599453)
    r = pltpu.reciprocal(u, approx=True)
    return jnp.maximum(pre, 0.0) + log, jnp.where(pre >= 0, r, t * r)


def encode_body(n, tm, fc, *refs):
    parts = refs[:n]
    enc_ref, b_ref, dec_ref, f_ref, s_ref, l_ref, n_ref = refs[n : n + 7]
    tot = None
    counted = 0.0
    at = 0
    for c_ref, p_ref in zip(parts, refs[n + 7 :]):
        for i in range(c_ref.shape[0] // tm):
            rows = slice(at, at + tm)
            at += tm
            c = c_ref[i * tm : (i + 1) * tm, :]
            out = c[:, 0:1].astype(F32) > 0.5 * SENTINEL
            off = jnp.where(out, -1e30, 0.0)
            counted += jnp.sum(jnp.where(out, 0.0, 1.0), axis=0, keepdims=True)
            acc = None
            for k in range(enc_ref.shape[1] // fc):
                sl = slice(k * fc, (k + 1) * fc)
                pre = jnp.dot(c, enc_ref[:, sl], preferred_element_type=F32) + b_ref[:, sl] + off
                feats, sig = activate(pre)
                low = feats.astype(BF)
                f_ref[rows, sl] = low
                s_ref[rows, sl] = sig.astype(BF)
                d = jnp.dot(low, dec_ref[sl, :], preferred_element_type=F32)
                acc = d if acc is None else acc + d
                part = jnp.sum(feats.reshape(-1, 8, fc), axis=0)
                part = sum(part[:, j * 128 : (j + 1) * 128] for j in range(fc // 128))
                tot = part if tot is None else tot + part
            p_ref[i * tm : (i + 1) * tm, :] = acc.astype(p_ref.dtype)
    l_ref[...] = tot
    n_ref[...] = jnp.broadcast_to(counted, n_ref.shape)


def encode(parts, enc, bias, dec, tm=384, fc=768):
    t = sum(c.shape[0] for c in parts)
    d, nf = enc.shape
    outs = [((t, nf), BF), ((t, nf), BF), ((8, 128), F32), ((8, d), F32)] + [(c.shape, BF) for c in parts]
    return local(functools.partial(encode_body, len(parts), tm, fc), outs, (*parts, enc, bias, dec))


def flatten(groups):
    arrays, spec = [], []
    for group in groups:
        spec.append([])
        for part in group:
            spec[-1].append([])
            for v, a, b in part:
                k = next((i for i, w in enumerate(arrays) if w is v), len(arrays))
                if k == len(arrays):
                    arrays.append(v)
                spec[-1][-1].append((k, a, b))
    return arrays, spec


def rows_of(refs, part, lanes=slice(None)):
    blocks = [refs[k][a:b, lanes] for k, a, b in part]
    return blocks[0] if len(blocks) == 1 else jnp.concatenate(blocks, 0)


def grad_dec_body(spec, n, has, start, fb, *refs):
    rest = refs[n:]
    out = rest[-1]
    for k in range(out.shape[0] // fb):
        sl = slice(start + k * fb, start + (k + 1) * fb)
        acc = rest[0][sl, :] if has else None
        for f, g in spec:
            d = lax.dot_general(rows_of(refs, f, sl), rows_of(refs, g), TN, preferred_element_type=F32)
            acc = d if acc is None else acc + d
        out[k * fb : (k + 1) * fb, :] = acc.astype(out.dtype)


def grad_dec(groups, acc, dtype, shape, start=0, size=None, fb=384):
    arrays, spec = flatten(groups)
    n = len(arrays)
    nf, d = shape
    size = nf if size is None else size
    has = acc is not None
    return local(
        functools.partial(grad_dec_body, spec, n, has, start, fb),
        [((size, d), dtype)],
        (*arrays, *([acc] * has)),
        aliases={n: 0} if has and dtype == F32 else {},
    )[0]


def grad_enc_body(spec, n, has, start, fb, *refs):
    dec, rest = refs[n], refs[n + 1 :]
    out, out_tot = rest[-2:]
    for k in range(out.shape[1] // fb):
        sl = slice(start + k * fb, start + (k + 1) * fb)
        ol = slice(k * fb, (k + 1) * fb)
        acc = rest[0][:, sl] if has else None
        tot = rest[1][:, sl] if has else None
        for s, g, c in spec:
            gf = lax.dot_general(rows_of(refs, g), dec[sl, :], NT, preferred_element_type=F32)
            gp = (gf + sparsity_cost) * rows_of(refs, s, sl).astype(F32)
            part = jnp.sum(gp, axis=0, keepdims=True)
            tot = part if tot is None else tot + part
            d = lax.dot_general(rows_of(refs, c), gp.astype(BF), TN, preferred_element_type=F32)
            acc = d if acc is None else acc + d
        out[:, ol] = acc.astype(out.dtype)
        out_tot[:, ol] = tot


def grad_enc(groups, dec, acc, tot, dtype, start=0, size=None, fb=384):
    arrays, spec = flatten(groups)
    n = len(arrays)
    nf, d = dec.shape
    size = nf if size is None else size
    has = acc is not None
    outs = [((d, size), dtype), ((1, size), F32)]
    aliases = {n + 1: 0, n + 2: 1} if has and dtype == F32 else {}
    args = (*arrays, dec, *([acc, tot] if has else []))
    return local(functools.partial(grad_enc_body, spec, n, has, start, fb), outs, args, aliases=aliases)


def split_body(bit_ref, *refs):
    send, keep = refs[-2:]
    rows = keep.shape[0]
    here = pl.multiple_of(bit_ref[0] * rows, rows)
    there = pl.multiple_of((1 - bit_ref[0]) * rows, rows)
    send[...] = sum(r[pl.ds(there, rows), :].astype(F32) for r in refs[:-2]).astype(BF)
    keep[...] = sum(r[pl.ds(here, rows), :].astype(F32) for r in refs[:-2])


def split_sum(arrays, bit):
    rows, d = arrays[0].shape
    return local(split_body, [((rows // 2, d), BF), ((rows // 2, d), F32)], arrays, (bit,))


def count_body(n_ref, out_ref, packed_ref):
    out_ref[...] = n_ref[...]
    packed_ref[...] = pack(n_ref[...])


def split_few_body(bit_ref, a_ref, got_ref, few_ref, send, keep, few_out):
    rows = keep.shape[0]
    here = pl.multiple_of(bit_ref[0] * rows, rows)
    there = pl.multiple_of((1 - bit_ref[0]) * rows, rows)
    few = few_ref[...] + unpack(got_ref[2 * rows :, :])
    few_out[...] = few
    sent = a_ref[pl.ds(there, rows), :].astype(F32) + got_ref[pl.ds(there, rows), :].astype(F32)
    send[:rows, :] = sent.astype(BF)
    send[rows:, :] = pack(few)
    keep[...] = a_ref[pl.ds(here, rows), :].astype(F32) + got_ref[pl.ds(here, rows), :].astype(F32)


def split_few(mine, got, few, bit):
    rows, d = mine.shape
    h = rows // 2
    outs = [((h + 16, d), BF), ((h, d), F32), (few.shape, F32)]
    return local(split_few_body, outs, (mine, got, few), (bit,))


def total_few_body(a_ref, got_ref, few_ref, out_ref, few_out):
    rows = a_ref.shape[0]
    out_ref[...] = (a_ref[...] + got_ref[:rows, :].astype(F32)).astype(BF)
    few_out[...] = few_ref[...] + unpack(got_ref[rows:, :])


def total_few(keep, got, few):
    return local(total_few_body, [(keep.shape, BF), (few.shape, F32)], (keep, got, few))


def bias_body(along_ref, few_ref, n_ref, *refs):
    row = lax.broadcasted_iota(jnp.int32, few_ref.shape, 0)
    few = jnp.where(row == 2, few_ref[...], along_ref[...])
    scale = 1.0 / n_ref[:1, :1]
    outs = refs[6:]
    for k, (row, rate) in enumerate(((2, 2.0), (0, 0.1))):
        master, moment, average = (r[...][None, :] for r in refs[3 * k : 3 * k + 3])
        made = advance(master, moment, average, few[row : row + 1, :] * scale, rate, False)
        for out, v in zip(outs[3 * k : 3 * k + 3], made):
            out[...] = v[0]
    outs[6][...] = few[1:2, :1]
    outs[7][...] = n_ref[:1, :1]


def bias_update(along, few, count, enc, dec):
    vmem = pl.BlockSpec(memory_space=pltpu.VMEM)
    return pl.pallas_call(
        bias_body,
        in_specs=[vmem] * 9,
        out_specs=[vmem] * 8,
        out_shape=[jax.ShapeDtypeStruct(v.shape, F32) for v in (*enc, *dec)] + [jax.ShapeDtypeStruct((1, 1), F32)] * 2,
        compiler_params=pltpu.CompilerParams(vmem_limit_bytes=4 * 2**20),
        cost_estimate=COST,
    )(along, few, count, *enc, *dec)


def update_body(rate, rows_unit, order_ref, n_ref, g_ref, w_ref, m_ref, a_ref, *refs):
    w_out, m_out, a_out = refs[-3:]
    g = g_ref[...].astype(F32) * (1.0 / n_ref[:1, :1])
    w_out[...], m_out[...], a_out[...] = advance(w_ref[...], m_ref[...], a_ref[...], g, rate, rows_unit)


def update(g, order, count, weights, rate, rows_unit, made=None):
    q, d = weights[0].shape[0] // 4, g.shape[1]
    there = pl.BlockSpec((q, d), lambda i, order: (order[i], 0))
    return pl.pallas_call(
        functools.partial(update_body, rate, rows_unit),
        grid_spec=pltpu.PrefetchScalarGridSpec(
            num_scalar_prefetch=1,
            grid=(2,),
            in_specs=[
                pl.BlockSpec((8, d), lambda i, order: (0, 0)),
                pl.BlockSpec((q, d), lambda i, order: (i, 0)),
                there,
                there,
                there,
            ]
            + ([pl.BlockSpec(memory_space=pl.ANY)] * 3 if made else []),
            out_specs=[there] * 3,
        ),
        out_shape=[jax.ShapeDtypeStruct(weights[0].shape, F32)] * 3,
        input_output_aliases={6: 0, 7: 1, 8: 2} if made else {},
        compiler_params=pltpu.CompilerParams(dimension_semantics=("arbitrary",), vmem_limit_bytes=14 * 2**20),
        cost_estimate=COST,
    )(
        order,
        count,
        pltpu.with_memory_space_constraint(g, pltpu.VMEM),
        *weights,
        *(made or []),
    )


def advance(master, moment, average, grad, rate, rows_unit):
    moment_new = momentum_rate * moment + grad
    master_new = master - rate * (grad + momentum_rate * moment_new)
    if rows_unit:
        master_new = master_new * lax.rsqrt(jnp.sum(master_new * master_new, axis=1, keepdims=True) + 1e-06)
    return (master_new, moment_new, average_rate * average + (1.0 - average_rate) * master_new)


def on_device(
    acts,
    valid,
    enc_master,
    enc_bias,
    dec_master,
    dec_bias,
    enc_moment,
    enc_bias_moment,
    dec_moment,
    dec_bias_moment,
    enc_average,
    enc_bias_average,
    dec_average,
    dec_bias_average,
):
    q, width = acts.shape
    heads = width // HEAD
    z = lax.axis_index("dp")
    core = lax.rem(lax.axis_index("feat"), 2)
    high = z // 2
    mixed = lax.rem(z + high, 2)
    bit_1 = jnp.where(core == 0, mixed, high)
    bit_2 = jnp.where(core == 0, high, mixed)
    bit_1 = bit_1.astype(jnp.int32)[None]
    bit_2 = bit_2.astype(jnp.int32)[None]
    valid_row = valid[None]
    bias_row = dec_bias[None]
    order_1 = jnp.concatenate([bit_1 * 2 + bit_2, bit_1 * 2 + 1 - bit_2])
    order_2 = jnp.concatenate([(1 - bit_1) * 2 + bit_2, (1 - bit_1) * 2 + 1 - bit_2])
    acts = after(acts, bit_1, bit_2, order_1, order_2)
    centered = center(acts, valid, dec_bias)

    n = enc_master.shape[1]
    both = jnp.concatenate([enc_master.astype(BF), dec_master.astype(BF)], 0)
    weights = {}

    def first_group(own):
        other = swap(after(both, own), 1)
        weights["enc"] = jnp.concatenate([both[:width], other[:width]], 1)
        weights["dec"] = jnp.concatenate([both[width:], other[width:]], 0)
        weights["bias"] = jnp.concatenate([enc_bias, swap(after(enc_bias, own), 1)], 0)[None, :]
        weights["made"] = encode([own], weights["enc"], weights["bias"], weights["dec"])
        return [weights["made"][3]]

    c_own, c_p, c_m, c_top, c_bottom = spread(centered, first_group, True)
    enc_two, dec_two, bias_two = weights["enc"], weights["dec"], weights["bias"]
    h = 2 * q
    f_own, s_own, l_own, n_own, y_own = weights["made"]
    f_t, s_t, l_t, n_t, y_pt, y_mt = encode([c_p[0][:h], c_m[0][:h]], enc_two, bias_two, dec_two)
    rest = after([stack((c_p[0], h, h + q), c_p[1]), stack((c_m[0], h, h + q), c_m[1])], n_t)
    f_b, s_b, l_b, n_b, y_pb, y_mb = encode(rest, enc_two, bias_two, dec_two)
    f_ft, s_ft, l_ft, n_ft, y_ft = encode([after(c_top, n_b)], enc_two, bias_two, dec_two)
    near_t = near_sum(y_own, move(y_pt, OUTER, 3), move(y_mt, OUTER, 1), 0)
    f_fb, s_fb, l_fb, n_fb, y_fb = encode([after(c_bottom, n_ft, near_t)], enc_two, bias_two, dec_two)
    near_b = near_sum(y_own, move(y_pb, OUTER, 3), move(y_mb, OUTER, 1), h)
    far_t = move(y_ft, OUTER, 2)
    far_b = move(y_fb, OUTER, 2)

    count = n_own + n_t + n_b + n_fb + n_ft
    sparse = l_own + l_t + l_b + l_fb + l_ft

    mine, to_p = outer_sum(near_t, after(far_t, sparse), F32)
    to_m, to_far = outer_sum(near_b, after(far_b, to_p), BF)
    got = direct_scatter(to_p, to_m, to_far, INNER)
    g_block, few = local(
        error_body,
        [((q, width), BF), ((8, width), F32)],
        (mine, *got, acts, valid_row, bias_row, sparse),
    )

    def all_rows(*arrays):
        return [(v, 0, v.shape[0]) for v in arrays]

    shape = dec_two.shape
    sums = {}

    def own_grads(own):
        sums["d"] = grad_dec([(all_rows(f_own), all_rows(own))], None, F32, shape)
        sums["e"], e_tot = grad_enc([(all_rows(s_own), all_rows(own), all_rows(c_own))], dec_two, None, None, F32)
        sums["t"] = e_tot
        return e_tot, sums["d"]

    g_own, g_p, g_m, g_top, g_bottom = spread(g_block, own_grads, False)
    d_sum, e_sum, e_tot = sums["d"], sums["e"], sums["t"]
    from_p = [(s_t, 0, h), (s_b, 0, h)], all_rows(*g_p), all_rows(*c_p)
    from_m = [(s_t, h, 2 * h), (s_b, h, 2 * h)], all_rows(*g_m), all_rows(*c_m)
    e_sum, e_tot = grad_enc([from_p, from_m], dec_two, e_sum, e_tot, F32)
    g_top, g_bottom = after([g_top, g_bottom], e_tot)

    def e_far(after_what):
        top, bottom = after([g_top, g_bottom], after_what)
        return [(all_rows(s_ft, s_fb), all_rows(top, bottom), all_rows(c_top, c_bottom))]

    count, count_packed = local(count_body, [(count.shape, F32), ((16, width), BF)], (count,))
    e_other, t_other = grad_enc(e_far((e_tot, count_packed)), dec_two, e_sum, e_tot, BF, n, n)
    e_got = swap(stack(e_other, count_packed), 1)
    e_mine, t_mine = grad_enc(e_far(t_other), dec_two, e_sum, e_tot, BF, 0, n)
    e_send, e_keep, count = split_few(e_mine, e_got, count, bit_1)

    def d_groups(after_what):
        p, m, top, bottom = after([g_p, g_m, g_top, g_bottom], after_what)
        return [
            ([(f_t, 0, h), (f_b, 0, h)], all_rows(*p)),
            ([(f_t, h, 2 * h), (f_b, h, 2 * h)], all_rows(*m)),
            (all_rows(f_ft, f_fb), all_rows(top, bottom)),
        ]

    few, few_other = small_sums(after(few, e_keep), t_mine, t_other, enc_two)
    d_other = grad_dec(d_groups(few_other), d_sum, BF, shape, n, n)
    d_got = swap(stack(d_other, few_other), 1)
    d_mine = grad_dec(d_groups(d_other), d_sum, BF, shape, 0, n)
    d_send, d_keep, few = split_few(d_mine, d_got, few, bit_1)

    enc_weights = enc_master, enc_moment, enc_average
    dec_weights = dec_master, dec_moment, dec_average
    e_send, e_keep, count = split_few(e_keep, after(trade(e_send, 0), d_send), count, bit_2)
    d_send, d_keep, few = split_few(d_keep, after(trade(d_send, 0), e_send), few, bit_2)
    e_total, count = total_few(e_keep, after(trade(e_send, 1), d_send), count)
    d_total, few = total_few(d_keep, after(trade(d_send, 1), e_total), few)
    e_half = stack(e_total, after(trade(e_total, 1), d_total))
    enc_made = update(e_half, order_1, count, enc_weights, 0.3, False)
    along = ring_total(few, ("x", "x"), enc_made[0])
    d_half = stack(d_total, after(trade(d_total, 1), along))
    dec_made = update(d_half, order_1, count, dec_weights, 0.3, True)
    along = ring_total(along, ("y", "y"), dec_made[0])
    enc_new, enc_moment_new, enc_average_new = update(
        after(trade(e_half, 0), along), order_2, count, enc_weights, 0.3, False, enc_made
    )
    d_near = after(trade(d_half, 0), enc_new)
    (
        enc_bias_new,
        enc_bias_moment_new,
        enc_bias_average_new,
        dec_bias_new,
        dec_bias_moment_new,
        dec_bias_average_new,
        loss_sum,
        total_count,
    ) = bias_update(
        along,
        few,
        count,
        (enc_bias, enc_bias_moment, enc_bias_average),
        (dec_bias, dec_bias_moment, dec_bias_average),
    )
    d_near = after(d_near, loss_sum)
    dec_new, dec_moment_new, dec_average_new = update(d_near, order_2, count, dec_weights, 0.3, True, dec_made)
    loss_sum = jnp.reshape(loss_sum, ())
    count = jnp.reshape(total_count, ())
    return (
        loss_sum,
        count,
        enc_new,
        enc_bias_new,
        dec_new,
        dec_bias_new,
        enc_moment_new,
        enc_bias_moment_new,
        dec_moment_new,
        dec_bias_moment_new,
        enc_average_new,
        enc_bias_average_new,
        dec_average_new,
        dec_bias_average_new,
    )


def solution(mesh):
    placed = (
        P(("dp", "feat"), None),
        P(("dp", "feat")),
        P(None, "feat"),
        P("feat"),
        P("feat", None),
        P(),
        P(None, "feat"),
        P("feat"),
        P("feat", None),
        P(),
        P(None, "feat"),
        P("feat"),
        P("feat", None),
        P(),
    )
    return jax.shard_map(
        on_device,
        mesh=mesh,
        in_specs=placed,
        out_specs=(
            P(),
            P(),
            P(None, "feat"),
            P("feat"),
            P("feat", None),
            P(),
            P(None, "feat"),
            P("feat"),
            P("feat", None),
            P(),
            P(None, "feat"),
            P("feat"),
            P("feat", None),
            P(),
        ),
        check_vma=False,
    )
```

```python
import functools
import itertools

import jax
import jax.numpy as jnp
from jax import lax
from jax.experimental import pallas as pl
from jax.experimental.pallas import tpu as pltpu
from jax.sharding import PartitionSpec as P

HEAD = 64
F32 = jnp.float32
BF = jnp.bfloat16

sparsity_cost = 0.2
momentum_rate = 0.9
average_rate = 0.8

AXES = ("dp", "feat")
DEPTH = ("z", "z")
SENTINEL = 1000.0
TN = (((0,), (0,)), ((), ()))
NT = (((1,), (1,)), ((), ()))
COST = pl.CostEstimate(flops=10**6, bytes_accessed=10**3, transcendentals=0)


def step_pairs(first, second, shift):
    pairs = []
    for z, y, x, c in itertools.product(range(4), range(4), range(4), range(2)):
        at = {"z": z, "y": y, "x": x}
        axis = first if c == 0 else second
        to = dict(at)
        to[axis] = (at[axis] + (-shift if axis == "y" else shift)) % 4
        pairs.append((((z * 4 + y) * 4 + x) * 2 + c, ((to["z"] * 4 + to["y"]) * 4 + to["x"]) * 2 + c))
    return pairs


def move(v, axes, shift):
    return lax.ppermute(v, AXES, step_pairs(axes[0], axes[1], shift))


def swap(v, bit):
    return lax.ppermute(v, AXES, [(i, i ^ bit) for i in range(128)])


INNER = ("x", "y")
OUTER = ("y", "x")
NEAR = ((1, 3), (3, 1))


def trade(v, which):
    pairs = []
    for i in range(128):
        z, rest = divmod(i, 32)
        pairs.append((i, (z ^ NEAR[rest % 2][which]) * 32 + rest))
    return lax.ppermute(v, AXES, pairs)


def after(x, *deps):
    return lax.optimization_barrier((x,) + deps)[0]


def direct_gather(block, axes):
    return move(block, axes, 1), move(block, axes, 3), move(block, axes, 2)


def direct_scatter(p, m, far, axes):
    return move(p, axes, 3), move(m, axes, 1), move(far, axes, 2)


def spread(block, between, early):
    q = block.shape[0]
    p, m, far = direct_gather(block, INNER)
    if not early:
        own = stack(block, p, m, far)
        p, m = move(own, OUTER, 1), move(own, OUTER, 3)
        p, m = after((p, m), *between(own))
        return own, [p], [m], move(p[: 2 * q], OUTER, 1), move(m[2 * q :], OUTER, 3)
    first = stack(block, p, m)
    p_1, m_1 = move(first, OUTER, 1), move(first, OUTER, 3)
    own = stack(first, far)
    p_2, m_2 = move(far, OUTER, 1), move(far, OUTER, 3)
    p_1, m_1 = after((p_1, m_1), *between(own))
    top_rows = p_1[: 2 * q]
    top = move(top_rows, OUTER, 1)
    p_2, m_2 = after((p_2, m_2), top_rows)
    bottom = move(stack((m_1, 2 * q, 3 * q), m_2), OUTER, 3)
    return own, [p_1, p_2], [m_1, m_2], top, bottom


def ring_total(v, axes, *deps):
    p, m, far = direct_gather(v, axes)
    if deps:
        p, m, far = after((p, m, far), *deps)
    return (v + far) + (p + m)


def local(body, outs, args, scalars=(), aliases=None, mib=8):
    vmem = pl.BlockSpec(memory_space=pltpu.VMEM)
    return pl.pallas_call(
        body,
        in_specs=[pl.BlockSpec(memory_space=pltpu.SMEM)] * len(scalars) + [vmem] * len(args),
        out_specs=[vmem] * len(outs),
        out_shape=[pltpu.VMEM(shape, dtype) for shape, dtype in outs],
        input_output_aliases=aliases or {},
        compiler_params=pltpu.CompilerParams(vmem_limit_bytes=mib * 2**20),
        cost_estimate=COST,
    )(*scalars, *[pltpu.with_memory_space_constraint(v, pltpu.VMEM) for v in args])


def center_body(a_hbm, v_hbm, b_hbm, c_ref, a_ref, v_ref, b_ref, sems):
    pairs = ((a_hbm, a_ref), (v_hbm, v_ref), (b_hbm, b_ref))
    copies = [pltpu.make_async_copy(s, d, sems.at[i]) for i, (s, d) in enumerate(pairs)]
    for copy in copies:
        copy.start()
    for copy in copies:
        copy.wait()
    n = a_ref.shape[0]
    same = lax.broadcasted_iota(jnp.int32, (n, n), 0) == lax.broadcasted_iota(jnp.int32, (n, n), 1)
    flag = jnp.sum(jnp.where(same, v_ref[...].astype(F32)[None, :], 0.0), axis=1, keepdims=True)
    c_ref[...] = jnp.where(flag > 0.5, a_ref[...].astype(F32) - b_ref[...][None, :], SENTINEL).astype(BF)


def center(acts, valid, bias):
    args = (acts, valid, bias)
    return pl.pallas_call(
        center_body,
        in_specs=[pl.BlockSpec(memory_space=pl.ANY)] * 3,
        out_specs=pl.BlockSpec(memory_space=pltpu.VMEM),
        out_shape=pltpu.VMEM(acts.shape, BF),
        scratch_shapes=[pltpu.VMEM(v.shape, v.dtype) for v in args] + [pltpu.SemaphoreType.DMA((3,))],
        compiler_params=pltpu.CompilerParams(vmem_limit_bytes=4 * 2**20),
        cost_estimate=COST,
    )(*[pltpu.with_memory_space_constraint(v, pltpu.HBM) for v in args])


def stack_body(ranges, *refs):
    at = 0
    for r, (a, b) in zip(refs, ranges):
        refs[-1][at : at + b - a, :] = r[a:b, :]
        at += b - a


def stack(*arrays):
    parts = [v if isinstance(v, tuple) else (v, 0, v.shape[0]) for v in arrays]
    ranges = [(a, b) for _, a, b in parts]
    arrays = [v for v, _, _ in parts]
    shape = (sum(b - a for a, b in ranges), arrays[0].shape[1])
    return local(functools.partial(stack_body, ranges), [(shape, arrays[0].dtype)], arrays)[0]


def total_body(a_ref, b_ref, out_ref):
    out_ref[...] = (a_ref[...].astype(F32) + b_ref[...].astype(F32)).astype(BF)


def total_low(a, b):
    return local(total_body, [(a.shape, BF)], (a, b))[0]


def near_body(at, y_ref, p_ref, m_ref, out_ref):
    rows = slice(at, at + out_ref.shape[0])
    out_ref[...] = y_ref[rows, :].astype(F32) + (p_ref[...].astype(F32) + m_ref[...].astype(F32))


def near_sum(y, p, m, at):
    return local(functools.partial(near_body, at), [(p.shape, F32)], (y, p, m))[0]


def halves_body(s_ref, f_ref, *out_refs):
    q = out_refs[0].shape[0]
    for k, out in enumerate(out_refs):
        rows = slice(k * q, (k + 1) * q)
        out[...] = (s_ref[rows, :] + f_ref[rows, :].astype(F32)).astype(out.dtype)


def outer_sum(near, far, dtype):
    rows, d = far.shape
    return local(halves_body, [((rows // 2, d), dtype), ((rows // 2, d), BF)], (near, far))


def error_body(m_ref, p_ref, n_ref, f_ref, a_ref, v_ref, b_ref, l_ref, g_ref, few_ref):
    n, d = a_ref.shape
    same = lax.broadcasted_iota(jnp.int32, (n, n), 0) == lax.broadcasted_iota(jnp.int32, (n, n), 1)
    flag = jnp.sum(jnp.where(same, v_ref[...].astype(F32), 0.0), axis=1, keepdims=True)
    head = (lax.broadcasted_iota(jnp.int32, (1, d), 1) // HEAD).astype(F32)
    weight = 0.5 + head / (d // HEAD - 1)
    decoded = m_ref[...] + (p_ref[...].astype(F32) + n_ref[...].astype(F32) + f_ref[...].astype(F32))
    err = decoded + b_ref[...] - a_ref[...].astype(F32)
    part = flag * weight * err
    direct = 2.0 * part
    g_ref[...] = direct.astype(BF)
    loss = jnp.sum(jnp.sum(part * err, axis=0, keepdims=True), axis=1, keepdims=True)
    loss += sparsity_cost * jnp.sum(jnp.sum(l_ref[...], axis=0, keepdims=True), axis=1, keepdims=True)
    row = lax.broadcasted_iota(jnp.int32, (8, d), 0)
    few_ref[...] = jnp.where(row == 0, jnp.sum(direct, axis=0, keepdims=True), jnp.where(row == 1, loss, 0.0))


def terms(v):
    high = v.astype(BF).astype(F32)
    mid = (v - high).astype(BF).astype(F32)
    return high, mid, v - high - mid


def pack(few):
    row = lax.broadcasted_iota(jnp.int32, (16, few.shape[1]), 0)
    out = jnp.zeros((16, few.shape[1]), F32)
    for k in range(3):
        for j, t in enumerate(terms(few[k : k + 1, :])):
            out = jnp.where(row == 3 * j + k, t, out)
    return out.astype(BF)


def unpack(packed):
    v = packed.astype(F32)
    row = lax.broadcasted_iota(jnp.int32, v.shape, 0)
    out_row = lax.broadcasted_iota(jnp.int32, (8, v.shape[1]), 0)
    out = jnp.zeros((8, v.shape[1]), F32)
    for k in range(3):
        mine = (row == k) | (row == k + 3) | (row == k + 6)
        out = jnp.where(out_row == k, jnp.sum(jnp.where(mine, v, 0.0), axis=0, keepdims=True), out)
    return out


def through_body(few_ref, t_ref, u_ref, enc_ref, mine_ref, other_ref):
    n = t_ref.shape[1]
    row = lax.broadcasted_iota(jnp.int32, (16, n), 0)
    moved = None
    for k, r in enumerate((t_ref, u_ref)):
        high, mid, low = terms(r[...])
        lhs = jnp.where(row == 0, high, jnp.where(row == 1, mid, jnp.where(row == 2, low, 0.0))).astype(BF)
        v = lax.dot_general(lhs, enc_ref[:, k * n : (k + 1) * n], NT, preferred_element_type=F32)
        v = jnp.sum(v, axis=0, keepdims=True)
        moved = v if moved is None else moved + v
    row = lax.broadcasted_iota(jnp.int32, few_ref.shape, 0)
    few = few_ref[...] - jnp.where(row == 0, moved, 0.0)
    mine_ref[...] = jnp.where(row == 2, t_ref[...], few)
    other_ref[...] = jnp.where(row == 2, u_ref[...], few)


def small_sums(few, t_mine, t_other, enc):
    return local(through_body, [(few.shape, F32)] * 2, (few, t_mine, t_other, enc))


def activate(pre):
    t = jnp.exp2(jnp.abs(pre) * -1.4426950408889634)
    u = 1.0 + t
    log = jnp.where(t < 1e-3, t * (1.0 - 0.5 * t), jnp.log2(u) * 0.6931471805599453)
    r = pltpu.reciprocal(u, approx=True)
    return jnp.maximum(pre, 0.0) + log, jnp.where(pre >= 0, r, t * r)


def encode_body(n, tm, fc, *refs):
    parts = refs[:n]
    enc_ref, b_ref, dec_ref, f_ref, s_ref, l_ref, n_ref = refs[n : n + 7]
    tot = None
    counted = 0.0
    at = 0
    for c_ref, p_ref in zip(parts, refs[n + 7 :]):
        for i in range(c_ref.shape[0] // tm):
            rows = slice(at, at + tm)
            at += tm
            c = c_ref[i * tm : (i + 1) * tm, :]
            out = c[:, 0:1].astype(F32) > 0.5 * SENTINEL
            off = jnp.where(out, -1e30, 0.0)
            counted += jnp.sum(jnp.where(out, 0.0, 1.0), axis=0, keepdims=True)
            acc = None
            for k in range(enc_ref.shape[1] // fc):
                sl = slice(k * fc, (k + 1) * fc)
                pre = jnp.dot(c, enc_ref[:, sl], preferred_element_type=F32) + b_ref[:, sl] + off
                feats, sig = activate(pre)
                low = feats.astype(BF)
                f_ref[rows, sl] = low
                s_ref[rows, sl] = sig.astype(BF)
                d = jnp.dot(low, dec_ref[sl, :], preferred_element_type=F32)
                acc = d if acc is None else acc + d
                part = jnp.sum(feats.reshape(-1, 8, fc), axis=0)
                part = sum(part[:, j * 128 : (j + 1) * 128] for j in range(fc // 128))
                tot = part if tot is None else tot + part
            p_ref[i * tm : (i + 1) * tm, :] = acc.astype(p_ref.dtype)
    l_ref[...] = tot
    n_ref[...] = jnp.broadcast_to(counted, n_ref.shape)


def encode(parts, enc, bias, dec, tm=384, fc=768):
    t = sum(c.shape[0] for c in parts)
    d, nf = enc.shape
    outs = [((t, nf), BF), ((t, nf), BF), ((8, 128), F32), ((8, d), F32)] + [(c.shape, BF) for c in parts]
    return local(functools.partial(encode_body, len(parts), tm, fc), outs, (*parts, enc, bias, dec))


def flatten(groups):
    arrays, spec = [], []
    for group in groups:
        spec.append([])
        for part in group:
            spec[-1].append([])
            for v, a, b in part:
                k = next((i for i, w in enumerate(arrays) if w is v), len(arrays))
                if k == len(arrays):
                    arrays.append(v)
                spec[-1][-1].append((k, a, b))
    return arrays, spec


def rows_of(refs, part, lanes=slice(None)):
    blocks = [refs[k][a:b, lanes] for k, a, b in part]
    return blocks[0] if len(blocks) == 1 else jnp.concatenate(blocks, 0)


def grad_dec_body(spec, n, has, start, fb, *refs):
    rest = refs[n:]
    out = rest[-1]
    for k in range(out.shape[0] // fb):
        sl = slice(start + k * fb, start + (k + 1) * fb)
        acc = rest[0][sl, :] if has else None
        for f, g in spec:
            d = lax.dot_general(rows_of(refs, f, sl), rows_of(refs, g), TN, preferred_element_type=F32)
            acc = d if acc is None else acc + d
        out[k * fb : (k + 1) * fb, :] = acc.astype(out.dtype)


def grad_dec(groups, acc, dtype, shape, start=0, size=None, fb=768):
    arrays, spec = flatten(groups)
    n = len(arrays)
    nf, d = shape
    size = nf if size is None else size
    has = acc is not None
    return local(
        functools.partial(grad_dec_body, spec, n, has, start, fb),
        [((size, d), dtype)],
        (*arrays, *([acc] * has)),
        aliases={n: 0} if has and dtype == F32 else {},
    )[0]


def grad_enc_body(spec, n, has, start, fb, *refs):
    dec, rest = refs[n], refs[n + 1 :]
    out, out_tot = rest[-2:]
    for k in range(out.shape[1] // fb):
        sl = slice(start + k * fb, start + (k + 1) * fb)
        ol = slice(k * fb, (k + 1) * fb)
        acc = rest[0][:, sl] if has else None
        tot = rest[1][:, sl] if has else None
        for s, g, c in spec:
            gf = lax.dot_general(rows_of(refs, g), dec[sl, :], NT, preferred_element_type=F32)
            gp = (gf + sparsity_cost) * rows_of(refs, s, sl).astype(F32)
            part = jnp.sum(gp, axis=0, keepdims=True)
            tot = part if tot is None else tot + part
            d = lax.dot_general(rows_of(refs, c), gp.astype(BF), TN, preferred_element_type=F32)
            acc = d if acc is None else acc + d
        out[:, ol] = acc.astype(out.dtype)
        out_tot[:, ol] = tot


def grad_enc(groups, dec, acc, tot, dtype, start=0, size=None, fb=768):
    arrays, spec = flatten(groups)
    n = len(arrays)
    nf, d = dec.shape
    size = nf if size is None else size
    has = acc is not None
    outs = [((d, size), dtype), ((1, size), F32)]
    aliases = {n + 1: 0, n + 2: 1} if has and dtype == F32 else {}
    args = (*arrays, dec, *([acc, tot] if has else []))
    return local(functools.partial(grad_enc_body, spec, n, has, start, fb), outs, args, aliases=aliases)


def split_body(bit_ref, *refs):
    send, keep = refs[-2:]
    rows = keep.shape[0]
    here = pl.multiple_of(bit_ref[0] * rows, rows)
    there = pl.multiple_of((1 - bit_ref[0]) * rows, rows)
    send[...] = sum(r[pl.ds(there, rows), :].astype(F32) for r in refs[:-2]).astype(BF)
    keep[...] = sum(r[pl.ds(here, rows), :].astype(F32) for r in refs[:-2])


def split_sum(arrays, bit):
    rows, d = arrays[0].shape
    return local(split_body, [((rows // 2, d), BF), ((rows // 2, d), F32)], arrays, (bit,))


def count_body(n_ref, out_ref, packed_ref):
    out_ref[...] = n_ref[...]
    packed_ref[...] = pack(n_ref[...])


def split_few_body(bit_ref, a_ref, got_ref, few_ref, send, keep, few_out):
    rows = keep.shape[0]
    here = pl.multiple_of(bit_ref[0] * rows, rows)
    there = pl.multiple_of((1 - bit_ref[0]) * rows, rows)
    few = few_ref[...] + unpack(got_ref[2 * rows :, :])
    few_out[...] = few
    sent = a_ref[pl.ds(there, rows), :].astype(F32) + got_ref[pl.ds(there, rows), :].astype(F32)
    send[:rows, :] = sent.astype(BF)
    send[rows:, :] = pack(few)
    keep[...] = a_ref[pl.ds(here, rows), :].astype(F32) + got_ref[pl.ds(here, rows), :].astype(F32)


def split_few(mine, got, few, bit):
    rows, d = mine.shape
    h = rows // 2
    outs = [((h + 16, d), BF), ((h, d), F32), (few.shape, F32)]
    return local(split_few_body, outs, (mine, got, few), (bit,))


def split_pair_body(bit_ref, a_ref, got_ref, few_ref, few_got_ref, send, keep, few_out):
    rows = keep.shape[0]
    here = pl.multiple_of(bit_ref[0] * rows, rows)
    there = pl.multiple_of((1 - bit_ref[0]) * rows, rows)
    few = few_ref[...] + few_got_ref[...]
    few_out[...] = few
    sent = a_ref[pl.ds(there, rows), :].astype(F32) + got_ref[pl.ds(there, rows), :].astype(F32)
    send[:rows, :] = sent.astype(BF)
    send[rows:, :] = pack(few)
    keep[...] = a_ref[pl.ds(here, rows), :].astype(F32) + got_ref[pl.ds(here, rows), :].astype(F32)


def split_pair(mine, got, few, few_got, bit):
    rows, d = mine.shape
    h = rows // 2
    outs = [((h + 16, d), BF), ((h, d), F32), (few.shape, F32)]
    return local(split_pair_body, outs, (mine, got, few, few_got), (bit,))


def total_few_body(a_ref, got_ref, few_ref, out_ref, few_out):
    rows = a_ref.shape[0]
    out_ref[...] = (a_ref[...] + got_ref[:rows, :].astype(F32)).astype(BF)
    few_out[...] = few_ref[...] + unpack(got_ref[rows:, :])


def total_few(keep, got, few):
    return local(total_few_body, [(keep.shape, BF), (few.shape, F32)], (keep, got, few))


def bias_body(along_ref, few_ref, n_ref, *refs):
    row = lax.broadcasted_iota(jnp.int32, few_ref.shape, 0)
    few = jnp.where(row == 2, few_ref[...], along_ref[...])
    scale = 1.0 / n_ref[:1, :1]
    outs = refs[6:]
    for k, (row, rate) in enumerate(((2, 2.0), (0, 0.1))):
        master, moment, average = (r[...][None, :] for r in refs[3 * k : 3 * k + 3])
        made = advance(master, moment, average, few[row : row + 1, :] * scale, rate, False)
        for out, v in zip(outs[3 * k : 3 * k + 3], made):
            out[...] = v[0]
    outs[6][...] = few[1:2, :1]
    outs[7][...] = n_ref[:1, :1]


def bias_update(along, few, count, enc, dec):
    vmem = pl.BlockSpec(memory_space=pltpu.VMEM)
    return pl.pallas_call(
        bias_body,
        in_specs=[vmem] * 9,
        out_specs=[vmem] * 8,
        out_shape=[jax.ShapeDtypeStruct(v.shape, F32) for v in (*enc, *dec)] + [jax.ShapeDtypeStruct((1, 1), F32)] * 2,
        compiler_params=pltpu.CompilerParams(vmem_limit_bytes=4 * 2**20),
        cost_estimate=COST,
    )(along, few, count, *enc, *dec)


def update_body(rate, rows_unit, order_ref, n_ref, g_ref, w_ref, m_ref, a_ref, *refs):
    w_out, m_out, a_out = refs[-3:]
    g = g_ref[...].astype(F32) * (1.0 / n_ref[:1, :1])
    w_out[...], m_out[...], a_out[...] = advance(w_ref[...], m_ref[...], a_ref[...], g, rate, rows_unit)


def update(g, order, count, weights, rate, rows_unit, made=None):
    q, d = weights[0].shape[0] // 4, g.shape[1]
    there = pl.BlockSpec((q, d), lambda i, order: (order[i], 0))
    return pl.pallas_call(
        functools.partial(update_body, rate, rows_unit),
        grid_spec=pltpu.PrefetchScalarGridSpec(
            num_scalar_prefetch=1,
            grid=(2,),
            in_specs=[
                pl.BlockSpec((8, d), lambda i, order: (0, 0)),
                pl.BlockSpec((q, d), lambda i, order: (i, 0)),
                there,
                there,
                there,
            ]
            + ([pl.BlockSpec(memory_space=pl.ANY)] * 3 if made else []),
            out_specs=[there] * 3,
        ),
        out_shape=[jax.ShapeDtypeStruct(weights[0].shape, F32)] * 3,
        input_output_aliases={6: 0, 7: 1, 8: 2} if made else {},
        compiler_params=pltpu.CompilerParams(dimension_semantics=("arbitrary",), vmem_limit_bytes=14 * 2**20),
        cost_estimate=COST,
    )(
        order,
        count,
        pltpu.with_memory_space_constraint(g, pltpu.VMEM),
        *weights,
        *(made or []),
    )


def advance(master, moment, average, grad, rate, rows_unit):
    moment_new = momentum_rate * moment + grad
    master_new = master - rate * (grad + momentum_rate * moment_new)
    if rows_unit:
        master_new = master_new * lax.rsqrt(jnp.sum(master_new * master_new, axis=1, keepdims=True) + 1e-06)
    return (master_new, moment_new, average_rate * average + (1.0 - average_rate) * master_new)


def on_device(
    acts,
    valid,
    enc_master,
    enc_bias,
    dec_master,
    dec_bias,
    enc_moment,
    enc_bias_moment,
    dec_moment,
    dec_bias_moment,
    enc_average,
    enc_bias_average,
    dec_average,
    dec_bias_average,
):
    q, width = acts.shape
    heads = width // HEAD
    z = lax.axis_index("dp")
    core = lax.rem(lax.axis_index("feat"), 2)
    high = z // 2
    mixed = lax.rem(z + high, 2)
    bit_1 = jnp.where(core == 0, mixed, high)
    bit_2 = jnp.where(core == 0, high, mixed)
    bit_1 = bit_1.astype(jnp.int32)[None]
    bit_2 = bit_2.astype(jnp.int32)[None]
    valid_row = valid[None]
    bias_row = dec_bias[None]
    order_1 = jnp.concatenate([bit_1 * 2 + bit_2, bit_1 * 2 + 1 - bit_2])
    order_2 = jnp.concatenate([(1 - bit_1) * 2 + bit_2, (1 - bit_1) * 2 + 1 - bit_2])
    acts = after(acts, bit_1, bit_2, order_1, order_2)
    centered = center(acts, valid, dec_bias)

    n = enc_master.shape[1]
    both = jnp.concatenate([enc_master.astype(BF), dec_master.astype(BF)], 0)
    weights = {}

    def first_group(own):
        other = swap(after(both, own), 1)
        weights["enc"] = jnp.concatenate([both[:width], other[:width]], 1)
        weights["dec"] = jnp.concatenate([both[width:], other[width:]], 0)
        weights["bias"] = jnp.concatenate([enc_bias, swap(after(enc_bias, own), 1)], 0)[None, :]
        weights["made"] = encode([own], weights["enc"], weights["bias"], weights["dec"])
        return [weights["made"][3]]

    c_own, c_p, c_m, c_top, c_bottom = spread(centered, first_group, True)
    enc_two, dec_two, bias_two = weights["enc"], weights["dec"], weights["bias"]
    h = 2 * q
    f_own, s_own, l_own, n_own, y_own = weights["made"]
    f_t, s_t, l_t, n_t, y_pt, y_mt = encode([c_p[0][:h], c_m[0][:h]], enc_two, bias_two, dec_two)
    rest = after([stack((c_p[0], h, h + q), c_p[1]), stack((c_m[0], h, h + q), c_m[1])], n_t)
    f_b, s_b, l_b, n_b, y_pb, y_mb = encode(rest, enc_two, bias_two, dec_two)
    f_ft, s_ft, l_ft, n_ft, y_ft = encode([after(c_top, n_b)], enc_two, bias_two, dec_two)
    near_t = near_sum(y_own, move(y_pt, OUTER, 3), move(y_mt, OUTER, 1), 0)
    f_fb, s_fb, l_fb, n_fb, y_fb = encode([after(c_bottom, n_ft, near_t)], enc_two, bias_two, dec_two)
    near_b = near_sum(y_own, move(y_pb, OUTER, 3), move(y_mb, OUTER, 1), h)
    far_t = move(y_ft, OUTER, 2)
    far_b = move(y_fb, OUTER, 2)

    count = n_own + n_t + n_b + n_fb + n_ft
    sparse = l_own + l_t + l_b + l_fb + l_ft

    mine, to_p = outer_sum(near_t, after(far_t, sparse), F32)
    to_m, to_far = outer_sum(near_b, after(far_b, to_p), BF)
    got = direct_scatter(to_p, to_m, to_far, INNER)
    g_block, few = local(
        error_body,
        [((q, width), BF), ((8, width), F32)],
        (mine, *got, acts, valid_row, bias_row, sparse),
    )

    def all_rows(*arrays):
        return [(v, 0, v.shape[0]) for v in arrays]

    shape = dec_two.shape
    sums = {}

    def own_grads(own):
        sums["d"] = grad_dec([(all_rows(f_own), all_rows(own))], None, F32, shape)
        sums["e"], e_tot = grad_enc([(all_rows(s_own), all_rows(own), all_rows(c_own))], dec_two, None, None, F32)
        sums["t"] = e_tot
        return e_tot, sums["d"]

    g_own, g_p, g_m, g_top, g_bottom = spread(g_block, own_grads, False)
    d_sum, e_sum, e_tot = sums["d"], sums["e"], sums["t"]
    from_p = [(s_t, 0, h), (s_b, 0, h)], all_rows(*g_p), all_rows(*c_p)
    from_m = [(s_t, h, 2 * h), (s_b, h, 2 * h)], all_rows(*g_m), all_rows(*c_m)
    e_sum, e_tot = grad_enc([from_p, from_m], dec_two, e_sum, e_tot, F32, fb=512)
    g_top, g_bottom = after([g_top, g_bottom], e_tot)

    def e_far(after_what):
        top, bottom = after([g_top, g_bottom], after_what)
        return [(all_rows(s_ft, s_fb), all_rows(top, bottom), all_rows(c_top, c_bottom))]

    def d_groups(after_what):
        p, m, top, bottom = after([g_p, g_m, g_top, g_bottom], after_what)
        return [
            ([(f_t, 0, h), (f_b, 0, h)], all_rows(*p)),
            ([(f_t, h, 2 * h), (f_b, h, 2 * h)], all_rows(*m)),
            (all_rows(f_ft, f_fb), all_rows(top, bottom)),
        ]

    count, count_packed = local(count_body, [(count.shape, F32), ((16, width), BF)], (count,))
    d_other = grad_dec(d_groups(count_packed), d_sum, BF, shape, n, n)
    d_got = swap(d_other, 1)
    e_other, t_other = grad_enc(e_far((e_tot, d_other)), dec_two, e_sum, e_tot, BF, n, n)
    e_got = swap(stack(e_other, count_packed), 1)
    e_mine, t_mine = grad_enc(e_far(t_other), dec_two, e_sum, e_tot, BF, 0, n)
    e_send, e_keep, count = split_few(e_mine, e_got, count, bit_1)

    few, few_other = small_sums(after(few, e_keep), t_mine, t_other, enc_two)
    few_got = swap(few_other, 1)
    d_mine = grad_dec(d_groups(few_other), d_sum, BF, shape, 0, n)
    d_send, d_keep, few = split_pair(d_mine, d_got, few, few_got, bit_1)

    enc_weights = enc_master, enc_moment, enc_average
    dec_weights = dec_master, dec_moment, dec_average
    e_send, e_keep, count = split_few(e_keep, after(trade(e_send, 0), d_send), count, bit_2)
    d_send, d_keep, few = split_few(d_keep, after(trade(d_send, 0), e_send), few, bit_2)
    e_total, count = total_few(e_keep, after(trade(e_send, 1), d_send), count)
    d_total, few = total_few(d_keep, after(trade(d_send, 1), e_total), few)
    e_half = stack(e_total, after(trade(e_total, 1), d_total))
    enc_made = update(e_half, order_1, count, enc_weights, 0.3, False)
    along = ring_total(few, ("x", "x"), enc_made[0])
    d_half = stack(d_total, after(trade(d_total, 1), along))
    dec_made = update(d_half, order_1, count, dec_weights, 0.3, True)
    along = ring_total(along, ("y", "y"), dec_made[0])
    enc_new, enc_moment_new, enc_average_new = update(
        after(trade(e_half, 0), along), order_2, count, enc_weights, 0.3, False, enc_made
    )
    d_near = after(trade(d_half, 0), enc_new)
    (
        enc_bias_new,
        enc_bias_moment_new,
        enc_bias_average_new,
        dec_bias_new,
        dec_bias_moment_new,
        dec_bias_average_new,
        loss_sum,
        total_count,
    ) = bias_update(
        along,
        few,
        count,
        (enc_bias, enc_bias_moment, enc_bias_average),
        (dec_bias, dec_bias_moment, dec_bias_average),
    )
    d_near = after(d_near, loss_sum)
    dec_new, dec_moment_new, dec_average_new = update(d_near, order_2, count, dec_weights, 0.3, True, dec_made)
    loss_sum = jnp.reshape(loss_sum, ())
    count = jnp.reshape(total_count, ())
    return (
        loss_sum,
        count,
        enc_new,
        enc_bias_new,
        dec_new,
        dec_bias_new,
        enc_moment_new,
        enc_bias_moment_new,
        dec_moment_new,
        dec_bias_moment_new,
        enc_average_new,
        enc_bias_average_new,
        dec_average_new,
        dec_bias_average_new,
    )


def solution(mesh):
    placed = (
        P(("dp", "feat"), None),
        P(("dp", "feat")),
        P(None, "feat"),
        P("feat"),
        P("feat", None),
        P(),
        P(None, "feat"),
        P("feat"),
        P("feat", None),
        P(),
        P(None, "feat"),
        P("feat"),
        P("feat", None),
        P(),
    )
    return jax.shard_map(
        on_device,
        mesh=mesh,
        in_specs=placed,
        out_specs=(
            P(),
            P(),
            P(None, "feat"),
            P("feat"),
            P("feat", None),
            P(),
            P(None, "feat"),
            P("feat"),
            P("feat", None),
            P(),
            P(None, "feat"),
            P("feat"),
            P("feat", None),
            P(),
        ),
        check_vma=False,
    )
```

```python
import functools
import itertools

import jax
import jax.numpy as jnp
from jax import lax
from jax.experimental import pallas as pl
from jax.experimental.pallas import tpu as pltpu
from jax.sharding import PartitionSpec as P

HEAD = 64
F32 = jnp.float32
BF = jnp.bfloat16

sparsity_cost = 0.2
momentum_rate = 0.9
average_rate = 0.8

AXES = ("dp", "feat")
DEPTH = ("z", "z")
SENTINEL = 1000.0
TN = (((0,), (0,)), ((), ()))
NT = (((1,), (1,)), ((), ()))
COST = pl.CostEstimate(flops=10**6, bytes_accessed=10**3, transcendentals=0)


def step_pairs(first, second, shift):
    pairs = []
    for z, y, x, c in itertools.product(range(4), range(4), range(4), range(2)):
        at = {"z": z, "y": y, "x": x}
        axis = first if c == 0 else second
        to = dict(at)
        to[axis] = (at[axis] + (-shift if axis == "y" else shift)) % 4
        pairs.append((((z * 4 + y) * 4 + x) * 2 + c, ((to["z"] * 4 + to["y"]) * 4 + to["x"]) * 2 + c))
    return pairs


def move(v, axes, shift):
    return lax.ppermute(v, AXES, step_pairs(axes[0], axes[1], shift))


def swap(v, bit):
    return lax.ppermute(v, AXES, [(i, i ^ bit) for i in range(128)])


INNER = ("x", "y")
OUTER = ("y", "x")
NEAR = ((1, 3), (3, 1))


def trade(v, which):
    pairs = []
    for i in range(128):
        z, rest = divmod(i, 32)
        pairs.append((i, (z ^ NEAR[rest % 2][which]) * 32 + rest))
    return lax.ppermute(v, AXES, pairs)


def after(x, *deps):
    return lax.optimization_barrier((x,) + deps)[0]


def direct_gather(block, axes):
    return move(block, axes, 1), move(block, axes, 3), move(block, axes, 2)


def direct_scatter(p, m, far, axes):
    return move(p, axes, 3), move(m, axes, 1), move(far, axes, 2)


def spread(block, between, early):
    q = block.shape[0]
    p, m, far = direct_gather(block, INNER)
    if not early:
        own = stack(block, p, m, far)
        p, m = move(own, OUTER, 1), move(own, OUTER, 3)
        p, m = after((p, m), *between(own))
        return own, [p], [m], move(p[: 2 * q], OUTER, 1), move(m[2 * q :], OUTER, 3)
    first = stack(block, p, m)
    p_1, m_1 = move(first, OUTER, 1), move(first, OUTER, 3)
    own = stack(first, far)
    p_2, m_2 = move(far, OUTER, 1), move(far, OUTER, 3)
    p_1, m_1 = after((p_1, m_1), *between(own))
    top_rows = p_1[: 2 * q]
    top = move(top_rows, OUTER, 1)
    p_2, m_2 = after((p_2, m_2), top_rows)
    bottom = move(stack((m_1, 2 * q, 3 * q), m_2), OUTER, 3)
    return own, [p_1, p_2], [m_1, m_2], top, bottom


def ring_total(v, axes, *deps):
    p, m, far = direct_gather(v, axes)
    if deps:
        p, m, far = after((p, m, far), *deps)
    return (v + far) + (p + m)


def local(body, outs, args, scalars=(), aliases=None, mib=8):
    vmem = pl.BlockSpec(memory_space=pltpu.VMEM)
    return pl.pallas_call(
        body,
        in_specs=[pl.BlockSpec(memory_space=pltpu.SMEM)] * len(scalars) + [vmem] * len(args),
        out_specs=[vmem] * len(outs),
        out_shape=[pltpu.VMEM(shape, dtype) for shape, dtype in outs],
        input_output_aliases=aliases or {},
        compiler_params=pltpu.CompilerParams(vmem_limit_bytes=mib * 2**20),
        cost_estimate=COST,
    )(*scalars, *[pltpu.with_memory_space_constraint(v, pltpu.VMEM) for v in args])


def center_body(a_hbm, v_hbm, b_hbm, c_ref, a_ref, v_ref, b_ref, sems):
    pairs = ((a_hbm, a_ref), (v_hbm, v_ref), (b_hbm, b_ref))
    copies = [pltpu.make_async_copy(s, d, sems.at[i]) for i, (s, d) in enumerate(pairs)]
    for copy in copies:
        copy.start()
    for copy in copies:
        copy.wait()
    n = a_ref.shape[0]
    same = lax.broadcasted_iota(jnp.int32, (n, n), 0) == lax.broadcasted_iota(jnp.int32, (n, n), 1)
    flag = jnp.sum(jnp.where(same, v_ref[...].astype(F32)[None, :], 0.0), axis=1, keepdims=True)
    c_ref[...] = jnp.where(flag > 0.5, a_ref[...].astype(F32) - b_ref[...][None, :], SENTINEL).astype(BF)


def center(acts, valid, bias):
    args = (acts, valid, bias)
    return pl.pallas_call(
        center_body,
        in_specs=[pl.BlockSpec(memory_space=pl.ANY)] * 3,
        out_specs=pl.BlockSpec(memory_space=pltpu.VMEM),
        out_shape=pltpu.VMEM(acts.shape, BF),
        scratch_shapes=[pltpu.VMEM(v.shape, v.dtype) for v in args] + [pltpu.SemaphoreType.DMA((3,))],
        compiler_params=pltpu.CompilerParams(vmem_limit_bytes=4 * 2**20),
        cost_estimate=COST,
    )(*[pltpu.with_memory_space_constraint(v, pltpu.HBM) for v in args])


def stack_body(ranges, *refs):
    at = 0
    for r, (a, b) in zip(refs, ranges):
        refs[-1][at : at + b - a, :] = r[a:b, :]
        at += b - a


def stack(*arrays):
    parts = [v if isinstance(v, tuple) else (v, 0, v.shape[0]) for v in arrays]
    ranges = [(a, b) for _, a, b in parts]
    arrays = [v for v, _, _ in parts]
    shape = (sum(b - a for a, b in ranges), arrays[0].shape[1])
    return local(functools.partial(stack_body, ranges), [(shape, arrays[0].dtype)], arrays)[0]


def total_body(a_ref, b_ref, out_ref):
    out_ref[...] = (a_ref[...].astype(F32) + b_ref[...].astype(F32)).astype(BF)


def total_low(a, b):
    return local(total_body, [(a.shape, BF)], (a, b))[0]


def near_body(at, y_ref, p_ref, m_ref, out_ref):
    rows = slice(at, at + out_ref.shape[0])
    out_ref[...] = y_ref[rows, :].astype(F32) + (p_ref[...].astype(F32) + m_ref[...].astype(F32))


def near_sum(y, p, m, at):
    return local(functools.partial(near_body, at), [(p.shape, F32)], (y, p, m))[0]


def halves_body(s_ref, f_ref, *out_refs):
    q = out_refs[0].shape[0]
    for k, out in enumerate(out_refs):
        rows = slice(k * q, (k + 1) * q)
        out[...] = (s_ref[rows, :] + f_ref[rows, :].astype(F32)).astype(out.dtype)


def outer_sum(near, far, dtype):
    rows, d = far.shape
    return local(halves_body, [((rows // 2, d), dtype), ((rows // 2, d), BF)], (near, far))


def error_body(m_ref, p_ref, n_ref, f_ref, a_ref, v_ref, b_ref, l_ref, g_ref, few_ref):
    n, d = a_ref.shape
    same = lax.broadcasted_iota(jnp.int32, (n, n), 0) == lax.broadcasted_iota(jnp.int32, (n, n), 1)
    flag = jnp.sum(jnp.where(same, v_ref[...].astype(F32), 0.0), axis=1, keepdims=True)
    head = (lax.broadcasted_iota(jnp.int32, (1, d), 1) // HEAD).astype(F32)
    weight = 0.5 + head / (d // HEAD - 1)
    decoded = m_ref[...] + (p_ref[...].astype(F32) + n_ref[...].astype(F32) + f_ref[...].astype(F32))
    err = decoded + b_ref[...] - a_ref[...].astype(F32)
    part = flag * weight * err
    direct = 2.0 * part
    g_ref[...] = direct.astype(BF)
    loss = jnp.sum(jnp.sum(part * err, axis=0, keepdims=True), axis=1, keepdims=True)
    loss += sparsity_cost * jnp.sum(jnp.sum(l_ref[...], axis=0, keepdims=True), axis=1, keepdims=True)
    row = lax.broadcasted_iota(jnp.int32, (8, d), 0)
    few_ref[...] = jnp.where(row == 0, jnp.sum(direct, axis=0, keepdims=True), jnp.where(row == 1, loss, 0.0))


def terms(v):
    high = v.astype(BF).astype(F32)
    mid = (v - high).astype(BF).astype(F32)
    return high, mid, v - high - mid


def pack(few):
    row = lax.broadcasted_iota(jnp.int32, (16, few.shape[1]), 0)
    out = jnp.zeros((16, few.shape[1]), F32)
    for k in range(3):
        for j, t in enumerate(terms(few[k : k + 1, :])):
            out = jnp.where(row == 3 * j + k, t, out)
    return out.astype(BF)


def unpack(packed):
    v = packed.astype(F32)
    row = lax.broadcasted_iota(jnp.int32, v.shape, 0)
    out_row = lax.broadcasted_iota(jnp.int32, (8, v.shape[1]), 0)
    out = jnp.zeros((8, v.shape[1]), F32)
    for k in range(3):
        mine = (row == k) | (row == k + 3) | (row == k + 6)
        out = jnp.where(out_row == k, jnp.sum(jnp.where(mine, v, 0.0), axis=0, keepdims=True), out)
    return out


def through_body(few_ref, t_ref, u_ref, enc_ref, mine_ref, other_ref):
    n = t_ref.shape[1]
    row = lax.broadcasted_iota(jnp.int32, (16, n), 0)
    moved = None
    for k, r in enumerate((t_ref, u_ref)):
        high, mid, low = terms(r[...])
        lhs = jnp.where(row == 0, high, jnp.where(row == 1, mid, jnp.where(row == 2, low, 0.0))).astype(BF)
        v = lax.dot_general(lhs, enc_ref[:, k * n : (k + 1) * n], NT, preferred_element_type=F32)
        v = jnp.sum(v, axis=0, keepdims=True)
        moved = v if moved is None else moved + v
    row = lax.broadcasted_iota(jnp.int32, few_ref.shape, 0)
    few = few_ref[...] - jnp.where(row == 0, moved, 0.0)
    mine_ref[...] = jnp.where(row == 2, t_ref[...], few)
    other_ref[...] = jnp.where(row == 2, u_ref[...], few)


def small_sums(few, t_mine, t_other, enc):
    return local(through_body, [(few.shape, F32)] * 2, (few, t_mine, t_other, enc))


def activate(pre):
    t = jnp.exp2(jnp.abs(pre) * -1.4426950408889634)
    u = 1.0 + t
    log = jnp.where(t < 1e-3, t * (1.0 - 0.5 * t), jnp.log2(u) * 0.6931471805599453)
    r = pltpu.reciprocal(u, approx=True)
    return jnp.maximum(pre, 0.0) + log, jnp.where(pre >= 0, r, t * r)


def encode_body(n, tm, fc, *refs):
    parts = refs[:n]
    enc_ref, b_ref, dec_ref, f_ref, s_ref, l_ref, n_ref = refs[n : n + 7]
    tot = None
    counted = 0.0
    at = 0
    for c_ref, p_ref in zip(parts, refs[n + 7 :]):
        for i in range(c_ref.shape[0] // tm):
            rows = slice(at, at + tm)
            at += tm
            c = c_ref[i * tm : (i + 1) * tm, :]
            out = c[:, 0:1].astype(F32) > 0.5 * SENTINEL
            off = jnp.where(out, -1e30, 0.0)
            counted += jnp.sum(jnp.where(out, 0.0, 1.0), axis=0, keepdims=True)
            acc = None
            for k in range(enc_ref.shape[1] // fc):
                sl = slice(k * fc, (k + 1) * fc)
                pre = jnp.dot(c, enc_ref[:, sl], preferred_element_type=F32) + b_ref[:, sl] + off
                feats, sig = activate(pre)
                low = feats.astype(BF)
                f_ref[rows, sl] = low
                s_ref[rows, sl] = sig.astype(BF)
                d = jnp.dot(low, dec_ref[sl, :], preferred_element_type=F32)
                acc = d if acc is None else acc + d
                part = jnp.sum(feats.reshape(-1, 8, fc), axis=0)
                part = sum(part[:, j * 128 : (j + 1) * 128] for j in range(fc // 128))
                tot = part if tot is None else tot + part
            p_ref[i * tm : (i + 1) * tm, :] = acc.astype(p_ref.dtype)
    l_ref[...] = tot
    n_ref[...] = jnp.broadcast_to(counted, n_ref.shape)


def encode(parts, enc, bias, dec, tm=384, fc=768):
    t = sum(c.shape[0] for c in parts)
    d, nf = enc.shape
    outs = [((t, nf), BF), ((t, nf), BF), ((8, 128), F32), ((8, d), F32)] + [(c.shape, BF) for c in parts]
    return local(functools.partial(encode_body, len(parts), tm, fc), outs, (*parts, enc, bias, dec))


def flatten(groups):
    arrays, spec = [], []
    for group in groups:
        spec.append([])
        for part in group:
            spec[-1].append([])
            for v, a, b in part:
                k = next((i for i, w in enumerate(arrays) if w is v), len(arrays))
                if k == len(arrays):
                    arrays.append(v)
                spec[-1][-1].append((k, a, b))
    return arrays, spec


def rows_of(refs, part, lanes=slice(None)):
    blocks = [refs[k][a:b, lanes] for k, a, b in part]
    return blocks[0] if len(blocks) == 1 else jnp.concatenate(blocks, 0)


def grad_dec_body(spec, n, has, start, fb, *refs):
    rest = refs[n:]
    out = rest[-1]
    for k in range(out.shape[0] // fb):
        sl = slice(start + k * fb, start + (k + 1) * fb)
        acc = rest[0][sl, :] if has else None
        for f, g in spec:
            d = lax.dot_general(rows_of(refs, f, sl), rows_of(refs, g), TN, preferred_element_type=F32)
            acc = d if acc is None else acc + d
        out[k * fb : (k + 1) * fb, :] = acc.astype(out.dtype)


def grad_dec(groups, acc, dtype, shape, start=0, size=None, fb=768):
    arrays, spec = flatten(groups)
    n = len(arrays)
    nf, d = shape
    size = nf if size is None else size
    has = acc is not None
    return local(
        functools.partial(grad_dec_body, spec, n, has, start, fb),
        [((size, d), dtype)],
        (*arrays, *([acc] * has)),
        aliases={n: 0} if has and dtype == F32 else {},
    )[0]


def grad_enc_body(spec, n, has, start, fb, *refs):
    dec, rest = refs[n], refs[n + 1 :]
    out, out_tot = rest[-2:]
    for k in range(out.shape[1] // fb):
        sl = slice(start + k * fb, start + (k + 1) * fb)
        ol = slice(k * fb, (k + 1) * fb)
        acc = rest[0][:, sl] if has else None
        tot = rest[1][:, sl] if has else None
        for s, g, c in spec:
            gf = lax.dot_general(rows_of(refs, g), dec[sl, :], NT, preferred_element_type=F32)
            gp = (gf + sparsity_cost) * rows_of(refs, s, sl).astype(F32)
            part = jnp.sum(gp, axis=0, keepdims=True)
            tot = part if tot is None else tot + part
            d = lax.dot_general(rows_of(refs, c), gp.astype(BF), TN, preferred_element_type=F32)
            acc = d if acc is None else acc + d
        out[:, ol] = acc.astype(out.dtype)
        out_tot[:, ol] = tot


def grad_enc(groups, dec, acc, tot, dtype, start=0, size=None, fb=768):
    arrays, spec = flatten(groups)
    n = len(arrays)
    nf, d = dec.shape
    size = nf if size is None else size
    has = acc is not None
    outs = [((d, size), dtype), ((1, size), F32)]
    aliases = {n + 1: 0, n + 2: 1} if has and dtype == F32 else {}
    args = (*arrays, dec, *([acc, tot] if has else []))
    return local(functools.partial(grad_enc_body, spec, n, has, start, fb), outs, args, aliases=aliases)


def split_body(bit_ref, *refs):
    send, keep = refs[-2:]
    rows = keep.shape[0]
    here = pl.multiple_of(bit_ref[0] * rows, rows)
    there = pl.multiple_of((1 - bit_ref[0]) * rows, rows)
    send[...] = sum(r[pl.ds(there, rows), :].astype(F32) for r in refs[:-2]).astype(BF)
    keep[...] = sum(r[pl.ds(here, rows), :].astype(F32) for r in refs[:-2])


def split_sum(arrays, bit):
    rows, d = arrays[0].shape
    return local(split_body, [((rows // 2, d), BF), ((rows // 2, d), F32)], arrays, (bit,))


def count_body(n_ref, out_ref, packed_ref):
    out_ref[...] = n_ref[...]
    packed_ref[...] = pack(n_ref[...])


def split_few_body(bit_ref, a_ref, got_ref, few_ref, send, keep, few_out):
    rows = keep.shape[0]
    here = pl.multiple_of(bit_ref[0] * rows, rows)
    there = pl.multiple_of((1 - bit_ref[0]) * rows, rows)
    few = few_ref[...] + unpack(got_ref[2 * rows :, :])
    few_out[...] = few
    sent = a_ref[pl.ds(there, rows), :].astype(F32) + got_ref[pl.ds(there, rows), :].astype(F32)
    send[:rows, :] = sent.astype(BF)
    send[rows:, :] = pack(few)
    keep[...] = a_ref[pl.ds(here, rows), :].astype(F32) + got_ref[pl.ds(here, rows), :].astype(F32)


def split_few(mine, got, few, bit):
    rows, d = mine.shape
    h = rows // 2
    outs = [((h + 16, d), BF), ((h, d), F32), (few.shape, F32)]
    return local(split_few_body, outs, (mine, got, few), (bit,))


def split_pair_body(bit_ref, a_ref, got_ref, few_ref, few_got_ref, send, keep, few_out):
    rows = keep.shape[0]
    here = pl.multiple_of(bit_ref[0] * rows, rows)
    there = pl.multiple_of((1 - bit_ref[0]) * rows, rows)
    few = few_ref[...] + few_got_ref[...]
    few_out[...] = few
    sent = a_ref[pl.ds(there, rows), :].astype(F32) + got_ref[pl.ds(there, rows), :].astype(F32)
    send[:rows, :] = sent.astype(BF)
    send[rows:, :] = pack(few)
    keep[...] = a_ref[pl.ds(here, rows), :].astype(F32) + got_ref[pl.ds(here, rows), :].astype(F32)


def split_pair(mine, got, few, few_got, bit):
    rows, d = mine.shape
    h = rows // 2
    outs = [((h + 16, d), BF), ((h, d), F32), (few.shape, F32)]
    return local(split_pair_body, outs, (mine, got, few, few_got), (bit,))


def total_few_body(a_ref, got_ref, few_ref, out_ref, few_out):
    rows = a_ref.shape[0]
    out_ref[...] = (a_ref[...] + got_ref[:rows, :].astype(F32)).astype(BF)
    few_out[...] = few_ref[...] + unpack(got_ref[rows:, :])


def total_few(keep, got, few):
    return local(total_few_body, [(keep.shape, BF), (few.shape, F32)], (keep, got, few))


def bias_body(along_ref, few_ref, n_ref, *refs):
    row = lax.broadcasted_iota(jnp.int32, few_ref.shape, 0)
    few = jnp.where(row == 2, few_ref[...], along_ref[...])
    scale = 1.0 / n_ref[:1, :1]
    outs = refs[6:]
    for k, (row, rate) in enumerate(((2, 2.0), (0, 0.1))):
        master, moment, average = (r[...][None, :] for r in refs[3 * k : 3 * k + 3])
        made = advance(master, moment, average, few[row : row + 1, :] * scale, rate, False)
        for out, v in zip(outs[3 * k : 3 * k + 3], made):
            out[...] = v[0]
    outs[6][...] = few[1:2, :1]
    outs[7][...] = n_ref[:1, :1]


def bias_update(along, few, count, enc, dec):
    vmem = pl.BlockSpec(memory_space=pltpu.VMEM)
    return pl.pallas_call(
        bias_body,
        in_specs=[vmem] * 9,
        out_specs=[vmem] * 8,
        out_shape=[jax.ShapeDtypeStruct(v.shape, F32) for v in (*enc, *dec)] + [jax.ShapeDtypeStruct((1, 1), F32)] * 2,
        compiler_params=pltpu.CompilerParams(vmem_limit_bytes=4 * 2**20),
        cost_estimate=COST,
    )(along, few, count, *enc, *dec)


def update_body(rate, rows_unit, order_ref, n_ref, g_ref, w_ref, m_ref, a_ref, *refs):
    w_out, m_out, a_out = refs[-3:]
    g = g_ref[...].astype(F32) * (1.0 / n_ref[:1, :1])
    w_out[...], m_out[...], a_out[...] = advance(w_ref[...], m_ref[...], a_ref[...], g, rate, rows_unit)


def update(g, order, count, weights, rate, rows_unit, made=None):
    q, d = weights[0].shape[0] // 4, g.shape[1]
    there = pl.BlockSpec((q, d), lambda i, order: (order[i], 0))
    return pl.pallas_call(
        functools.partial(update_body, rate, rows_unit),
        grid_spec=pltpu.PrefetchScalarGridSpec(
            num_scalar_prefetch=1,
            grid=(2,),
            in_specs=[
                pl.BlockSpec((8, d), lambda i, order: (0, 0)),
                pl.BlockSpec((q, d), lambda i, order: (i, 0)),
                there,
                there,
                there,
            ]
            + ([pl.BlockSpec(memory_space=pl.ANY)] * 3 if made else []),
            out_specs=[there] * 3,
        ),
        out_shape=[jax.ShapeDtypeStruct(weights[0].shape, F32)] * 3,
        input_output_aliases={6: 0, 7: 1, 8: 2} if made else {},
        compiler_params=pltpu.CompilerParams(dimension_semantics=("arbitrary",), vmem_limit_bytes=14 * 2**20),
        cost_estimate=COST,
    )(
        order,
        count,
        pltpu.with_memory_space_constraint(g, pltpu.VMEM),
        *weights,
        *(made or []),
    )


def advance(master, moment, average, grad, rate, rows_unit):
    moment_new = momentum_rate * moment + grad
    master_new = master - rate * (grad + momentum_rate * moment_new)
    if rows_unit:
        master_new = master_new * lax.rsqrt(jnp.sum(master_new * master_new, axis=1, keepdims=True) + 1e-06)
    return (master_new, moment_new, average_rate * average + (1.0 - average_rate) * master_new)


def on_device(
    acts,
    valid,
    enc_master,
    enc_bias,
    dec_master,
    dec_bias,
    enc_moment,
    enc_bias_moment,
    dec_moment,
    dec_bias_moment,
    enc_average,
    enc_bias_average,
    dec_average,
    dec_bias_average,
):
    q, width = acts.shape
    heads = width // HEAD
    z = lax.axis_index("dp")
    core = lax.rem(lax.axis_index("feat"), 2)
    high = z // 2
    mixed = lax.rem(z + high, 2)
    bit_1 = jnp.where(core == 0, mixed, high)
    bit_2 = jnp.where(core == 0, high, mixed)
    bit_1 = bit_1.astype(jnp.int32)[None]
    bit_2 = bit_2.astype(jnp.int32)[None]
    valid_row = valid[None]
    bias_row = dec_bias[None]
    order_1 = jnp.concatenate([bit_1 * 2 + bit_2, bit_1 * 2 + 1 - bit_2])
    order_2 = jnp.concatenate([(1 - bit_1) * 2 + bit_2, (1 - bit_1) * 2 + 1 - bit_2])
    acts = after(acts, bit_1, bit_2, order_1, order_2)
    centered = center(acts, valid, dec_bias)

    n = enc_master.shape[1]
    both = jnp.concatenate([enc_master.astype(BF), dec_master.astype(BF)], 0)
    weights = {}

    def first_group(own):
        other = swap(after(both, own), 1)
        weights["enc"] = jnp.concatenate([both[:width], other[:width]], 1)
        weights["dec"] = jnp.concatenate([both[width:], other[width:]], 0)
        weights["bias"] = jnp.concatenate([enc_bias, swap(after(enc_bias, own), 1)], 0)[None, :]
        weights["made"] = encode([own], weights["enc"], weights["bias"], weights["dec"])
        return [weights["made"][3]]

    c_own, c_p, c_m, c_top, c_bottom = spread(centered, first_group, True)
    enc_two, dec_two, bias_two = weights["enc"], weights["dec"], weights["bias"]
    h = 2 * q
    f_own, s_own, l_own, n_own, y_own = weights["made"]
    f_t, s_t, l_t, n_t, y_pt, y_mt = encode([c_p[0][:h], c_m[0][:h]], enc_two, bias_two, dec_two)
    rest = after([stack((c_p[0], h, h + q), c_p[1]), stack((c_m[0], h, h + q), c_m[1])], n_t)
    f_b, s_b, l_b, n_b, y_pb, y_mb = encode(rest, enc_two, bias_two, dec_two)
    f_ft, s_ft, l_ft, n_ft, y_ft = encode([after(c_top, n_b)], enc_two, bias_two, dec_two)
    near_t = near_sum(y_own, move(y_pt, OUTER, 3), move(y_mt, OUTER, 1), 0)
    f_fb, s_fb, l_fb, n_fb, y_fb = encode([after(c_bottom, n_ft, near_t)], enc_two, bias_two, dec_two)
    near_b = near_sum(y_own, move(y_pb, OUTER, 3), move(y_mb, OUTER, 1), h)
    far_t = move(y_ft, OUTER, 2)
    far_b = move(y_fb, OUTER, 2)

    count = n_own + n_t + n_b + n_fb + n_ft
    sparse = l_own + l_t + l_b + l_fb + l_ft

    mine, to_p = outer_sum(near_t, after(far_t, sparse), F32)
    to_m, to_far = outer_sum(near_b, after(far_b, to_p), BF)
    got = direct_scatter(to_p, to_m, to_far, INNER)
    g_block, few = local(
        error_body,
        [((q, width), BF), ((8, width), F32)],
        (mine, *got, acts, valid_row, bias_row, sparse),
    )

    def all_rows(*arrays):
        return [(v, 0, v.shape[0]) for v in arrays]

    shape = dec_two.shape
    sums = {}

    def own_grads(own):
        sums["d"] = grad_dec([(all_rows(f_own), all_rows(own))], None, F32, shape)
        sums["e"], e_tot = grad_enc([(all_rows(s_own), all_rows(own), all_rows(c_own))], dec_two, None, None, F32)
        sums["t"] = e_tot
        return e_tot, sums["d"]

    g_own, g_p, g_m, g_top, g_bottom = spread(g_block, own_grads, False)
    d_sum, e_sum, e_tot = sums["d"], sums["e"], sums["t"]
    from_p = [(s_t, 0, h), (s_b, 0, h)], all_rows(*g_p), all_rows(*c_p)
    from_m = [(s_t, h, 2 * h), (s_b, h, 2 * h)], all_rows(*g_m), all_rows(*c_m)
    e_sum, e_tot = grad_enc([from_p, from_m], dec_two, e_sum, e_tot, F32, fb=512)
    g_top, g_bottom = after([g_top, g_bottom], e_tot)

    def e_far(after_what):
        top, bottom = after([g_top, g_bottom], after_what)
        return [(all_rows(s_ft, s_fb), all_rows(top, bottom), all_rows(c_top, c_bottom))]

    def d_groups(after_what):
        p, m, top, bottom = after([g_p, g_m, g_top, g_bottom], after_what)
        return [
            ([(f_t, 0, h), (f_b, 0, h)], all_rows(*p)),
            ([(f_t, h, 2 * h), (f_b, h, 2 * h)], all_rows(*m)),
            (all_rows(f_ft, f_fb), all_rows(top, bottom)),
        ]

    count, count_packed = local(count_body, [(count.shape, F32), ((16, width), BF)], (count,))
    d_other = grad_dec(d_groups(count_packed), d_sum, BF, shape, n, n)
    d_got = swap(d_other, 1)
    e_other, t_other = grad_enc(e_far((e_tot, d_other)), dec_two, e_sum, e_tot, BF, n, n)
    e_got = swap(stack(e_other, count_packed), 1)
    e_mine, t_mine = grad_enc(e_far(t_other), dec_two, e_sum, e_tot, BF, 0, n)
    e_send, e_keep, count = split_few(e_mine, e_got, count, bit_1)

    few, few_other = small_sums(after(few, e_keep), t_mine, t_other, enc_two)
    few_got = swap(few_other, 1)
    d_mine = grad_dec(d_groups(few_other), d_sum, BF, shape, 0, n)
    d_send, d_keep, few = split_pair(d_mine, d_got, few, few_got, bit_1)

    enc_weights = enc_master, enc_moment, enc_average
    dec_weights = dec_master, dec_moment, dec_average
    e_send, e_keep, count = split_few(e_keep, after(trade(e_send, 0), d_send), count, bit_2)
    d_send, d_keep, few = split_few(d_keep, after(trade(d_send, 0), e_send), few, bit_2)
    e_total, count = total_few(e_keep, after(trade(e_send, 1), d_send), count)
    d_total, few = total_few(d_keep, after(trade(d_send, 1), e_total), few)
    e_half = stack(e_total, after(trade(e_total, 1), d_total))
    enc_made = update(e_half, order_1, count, enc_weights, 0.3, False)
    along = ring_total(few, ("x", "x"), enc_made[0])
    d_half = stack(d_total, after(trade(d_total, 1), along))
    dec_made = update(d_half, order_1, count, dec_weights, 0.3, True)
    along = along + after(swap(along, 8), dec_made[0])
    enc_new, enc_moment_new, enc_average_new = update(
        after(trade(e_half, 0), along), order_2, count, enc_weights, 0.3, False, enc_made
    )
    along = along + after(swap(along, 24), enc_new)
    d_near = after(trade(d_half, 0), along)
    (
        enc_bias_new,
        enc_bias_moment_new,
        enc_bias_average_new,
        dec_bias_new,
        dec_bias_moment_new,
        dec_bias_average_new,
        loss_sum,
        total_count,
    ) = bias_update(
        along,
        few,
        count,
        (enc_bias, enc_bias_moment, enc_bias_average),
        (dec_bias, dec_bias_moment, dec_bias_average),
    )
    d_near = after(d_near, loss_sum)
    dec_new, dec_moment_new, dec_average_new = update(d_near, order_2, count, dec_weights, 0.3, True, dec_made)
    loss_sum = jnp.reshape(loss_sum, ())
    count = jnp.reshape(total_count, ())
    return (
        loss_sum,
        count,
        enc_new,
        enc_bias_new,
        dec_new,
        dec_bias_new,
        enc_moment_new,
        enc_bias_moment_new,
        dec_moment_new,
        dec_bias_moment_new,
        enc_average_new,
        enc_bias_average_new,
        dec_average_new,
        dec_bias_average_new,
    )


def solution(mesh):
    placed = (
        P(("dp", "feat"), None),
        P(("dp", "feat")),
        P(None, "feat"),
        P("feat"),
        P("feat", None),
        P(),
        P(None, "feat"),
        P("feat"),
        P("feat", None),
        P(),
        P(None, "feat"),
        P("feat"),
        P("feat", None),
        P(),
    )
    return jax.shard_map(
        on_device,
        mesh=mesh,
        in_specs=placed,
        out_specs=(
            P(),
            P(),
            P(None, "feat"),
            P("feat"),
            P("feat", None),
            P(),
            P(None, "feat"),
            P("feat"),
            P("feat", None),
            P(),
            P(None, "feat"),
            P("feat"),
            P("feat", None),
            P(),
        ),
        check_vma=False,
    )
```

```python
import functools
import itertools

import jax
import jax.numpy as jnp
from jax import lax
from jax.experimental import pallas as pl
from jax.experimental.pallas import tpu as pltpu
from jax.sharding import PartitionSpec as P

HEAD = 64
F32 = jnp.float32
BF = jnp.bfloat16

sparsity_cost = 0.2
momentum_rate = 0.9
average_rate = 0.8

AXES = ("dp", "feat")
DEPTH = ("z", "z")
SENTINEL = 1000.0
TN = (((0,), (0,)), ((), ()))
NT = (((1,), (1,)), ((), ()))
COST = pl.CostEstimate(flops=10**6, bytes_accessed=10**3, transcendentals=0)


def step_pairs(first, second, shift):
    pairs = []
    for z, y, x, c in itertools.product(range(4), range(4), range(4), range(2)):
        at = {"z": z, "y": y, "x": x}
        axis = first if c == 0 else second
        to = dict(at)
        to[axis] = (at[axis] + (-shift if axis == "y" else shift)) % 4
        pairs.append((((z * 4 + y) * 4 + x) * 2 + c, ((to["z"] * 4 + to["y"]) * 4 + to["x"]) * 2 + c))
    return pairs


def move(v, axes, shift):
    return lax.ppermute(v, AXES, step_pairs(axes[0], axes[1], shift))


def swap(v, bit):
    return lax.ppermute(v, AXES, [(i, i ^ bit) for i in range(128)])


INNER = ("x", "y")
OUTER = ("y", "x")
NEAR = ((1, 3), (3, 1))


def trade(v, which):
    pairs = []
    for i in range(128):
        z, rest = divmod(i, 32)
        pairs.append((i, (z ^ NEAR[rest % 2][which]) * 32 + rest))
    return lax.ppermute(v, AXES, pairs)


def after(x, *deps):
    return lax.optimization_barrier((x,) + deps)[0]


def direct_gather(block, axes):
    return move(block, axes, 1), move(block, axes, 3), move(block, axes, 2)


def direct_scatter(p, m, far, axes):
    far = move(far, axes, 2)
    m = move(m, axes, 1)
    return move(p, axes, 3), m, far


def spread(block, between, early):
    q = block.shape[0]
    p, m, far = direct_gather(block, INNER)
    if not early:
        own = stack(block, p, m, far)
        p, m = move(own, OUTER, 1), move(own, OUTER, 3)
        p, m = after((p, m), *between(own))
        return own, [p], [m], move(p[: 2 * q], OUTER, 1), move(m[2 * q :], OUTER, 3)
    first = stack(block, p, m)
    p_1, m_1 = move(first, OUTER, 1), move(first, OUTER, 3)
    own = stack(first, far)
    p_2, m_2 = move(far, OUTER, 1), move(far, OUTER, 3)
    p_1, m_1 = after((p_1, m_1), *between(own))
    top_rows = p_1[: 2 * q]
    top = move(top_rows, OUTER, 1)
    p_2, m_2 = after((p_2, m_2), top_rows)
    bottom = move(stack((m_1, 2 * q, 3 * q), m_2), OUTER, 3)
    return own, [p_1, p_2], [m_1, m_2], top, bottom


def ring_total(v, axes, *deps):
    p, m, far = direct_gather(v, axes)
    if deps:
        p, m, far = after((p, m, far), *deps)
    return (v + far) + (p + m)


def local(body, outs, args, scalars=(), aliases=None, mib=8):
    vmem = pl.BlockSpec(memory_space=pltpu.VMEM)
    return pl.pallas_call(
        body,
        in_specs=[pl.BlockSpec(memory_space=pltpu.SMEM)] * len(scalars) + [vmem] * len(args),
        out_specs=[vmem] * len(outs),
        out_shape=[pltpu.VMEM(shape, dtype) for shape, dtype in outs],
        input_output_aliases=aliases or {},
        compiler_params=pltpu.CompilerParams(vmem_limit_bytes=mib * 2**20),
        cost_estimate=COST,
    )(*scalars, *[pltpu.with_memory_space_constraint(v, pltpu.VMEM) for v in args])


def center_body(a_hbm, v_hbm, b_hbm, c_ref, a_ref, v_ref, b_ref, sems):
    pairs = ((a_hbm, a_ref), (v_hbm, v_ref), (b_hbm, b_ref))
    copies = [pltpu.make_async_copy(s, d, sems.at[i]) for i, (s, d) in enumerate(pairs)]
    for copy in copies:
        copy.start()
    for copy in copies:
        copy.wait()
    n = a_ref.shape[0]
    same = lax.broadcasted_iota(jnp.int32, (n, n), 0) == lax.broadcasted_iota(jnp.int32, (n, n), 1)
    flag = jnp.sum(jnp.where(same, v_ref[...].astype(F32)[None, :], 0.0), axis=1, keepdims=True)
    c_ref[...] = jnp.where(flag > 0.5, a_ref[...].astype(F32) - b_ref[...][None, :], SENTINEL).astype(BF)


def center(acts, valid, bias):
    args = (acts, valid, bias)
    return pl.pallas_call(
        center_body,
        in_specs=[pl.BlockSpec(memory_space=pl.ANY)] * 3,
        out_specs=pl.BlockSpec(memory_space=pltpu.VMEM),
        out_shape=pltpu.VMEM(acts.shape, BF),
        scratch_shapes=[pltpu.VMEM(v.shape, v.dtype) for v in args] + [pltpu.SemaphoreType.DMA((3,))],
        compiler_params=pltpu.CompilerParams(vmem_limit_bytes=4 * 2**20),
        cost_estimate=COST,
    )(*[pltpu.with_memory_space_constraint(v, pltpu.HBM) for v in args])


def stack_body(ranges, *refs):
    at = 0
    for r, (a, b) in zip(refs, ranges):
        refs[-1][at : at + b - a, :] = r[a:b, :]
        at += b - a


def stack(*arrays):
    parts = [v if isinstance(v, tuple) else (v, 0, v.shape[0]) for v in arrays]
    ranges = [(a, b) for _, a, b in parts]
    arrays = [v for v, _, _ in parts]
    shape = (sum(b - a for a, b in ranges), arrays[0].shape[1])
    return local(functools.partial(stack_body, ranges), [(shape, arrays[0].dtype)], arrays)[0]


def total_body(a_ref, b_ref, out_ref):
    out_ref[...] = (a_ref[...].astype(F32) + b_ref[...].astype(F32)).astype(BF)


def total_low(a, b):
    return local(total_body, [(a.shape, BF)], (a, b))[0]


def near_body(at, y_ref, p_ref, m_ref, out_ref):
    rows = slice(at, at + out_ref.shape[0])
    out_ref[...] = y_ref[rows, :].astype(F32) + (p_ref[...].astype(F32) + m_ref[...].astype(F32))


def near_sum(y, p, m, at):
    return local(functools.partial(near_body, at), [(p.shape, F32)], (y, p, m))[0]


def halves_body(s_ref, f_ref, *out_refs):
    q = out_refs[0].shape[0]
    for k, out in enumerate(out_refs):
        rows = slice(k * q, (k + 1) * q)
        out[...] = (s_ref[rows, :] + f_ref[rows, :].astype(F32)).astype(out.dtype)


def outer_sum(near, far, dtype):
    rows, d = far.shape
    return local(halves_body, [((rows // 2, d), dtype), ((rows // 2, d), BF)], (near, far))


def error_body(m_ref, p_ref, n_ref, f_ref, a_ref, v_ref, b_ref, l_ref, g_ref, few_ref):
    n, d = a_ref.shape
    same = lax.broadcasted_iota(jnp.int32, (n, n), 0) == lax.broadcasted_iota(jnp.int32, (n, n), 1)
    flag = jnp.sum(jnp.where(same, v_ref[...].astype(F32), 0.0), axis=1, keepdims=True)
    head = (lax.broadcasted_iota(jnp.int32, (1, d), 1) // HEAD).astype(F32)
    weight = 0.5 + head / (d // HEAD - 1)
    decoded = m_ref[...] + (p_ref[...].astype(F32) + n_ref[...].astype(F32) + f_ref[...].astype(F32))
    err = decoded + b_ref[...] - a_ref[...].astype(F32)
    part = flag * weight * err
    direct = 2.0 * part
    g_ref[...] = direct.astype(BF)
    loss = jnp.sum(jnp.sum(part * err, axis=0, keepdims=True), axis=1, keepdims=True)
    loss += sparsity_cost * jnp.sum(jnp.sum(l_ref[...], axis=0, keepdims=True), axis=1, keepdims=True)
    row = lax.broadcasted_iota(jnp.int32, (8, d), 0)
    few_ref[...] = jnp.where(row == 0, jnp.sum(direct, axis=0, keepdims=True), jnp.where(row == 1, loss, 0.0))


def terms(v):
    high = v.astype(BF).astype(F32)
    mid = (v - high).astype(BF).astype(F32)
    return high, mid, v - high - mid


def pack(few):
    row = lax.broadcasted_iota(jnp.int32, (16, few.shape[1]), 0)
    out = jnp.zeros((16, few.shape[1]), F32)
    for k in range(3):
        for j, t in enumerate(terms(few[k : k + 1, :])):
            out = jnp.where(row == 3 * j + k, t, out)
    return out.astype(BF)


def unpack(packed):
    v = packed.astype(F32)
    row = lax.broadcasted_iota(jnp.int32, v.shape, 0)
    out_row = lax.broadcasted_iota(jnp.int32, (8, v.shape[1]), 0)
    out = jnp.zeros((8, v.shape[1]), F32)
    for k in range(3):
        mine = (row == k) | (row == k + 3) | (row == k + 6)
        out = jnp.where(out_row == k, jnp.sum(jnp.where(mine, v, 0.0), axis=0, keepdims=True), out)
    return out


def through_body(few_ref, t_ref, u_ref, enc_ref, mine_ref, other_ref):
    n = t_ref.shape[1]
    row = lax.broadcasted_iota(jnp.int32, (16, n), 0)
    moved = None
    for k, r in enumerate((t_ref, u_ref)):
        high, mid, low = terms(r[...])
        lhs = jnp.where(row == 0, high, jnp.where(row == 1, mid, jnp.where(row == 2, low, 0.0))).astype(BF)
        v = lax.dot_general(lhs, enc_ref[:, k * n : (k + 1) * n], NT, preferred_element_type=F32)
        v = jnp.sum(v, axis=0, keepdims=True)
        moved = v if moved is None else moved + v
    row = lax.broadcasted_iota(jnp.int32, few_ref.shape, 0)
    few = few_ref[...] - jnp.where(row == 0, moved, 0.0)
    mine_ref[...] = jnp.where(row == 2, t_ref[...], few)
    other_ref[...] = jnp.where(row == 2, u_ref[...], few)


def small_sums(few, t_mine, t_other, enc):
    return local(through_body, [(few.shape, F32)] * 2, (few, t_mine, t_other, enc))


def activate(pre):
    t = jnp.exp2(jnp.abs(pre) * -1.4426950408889634)
    u = 1.0 + t
    log = jnp.where(t < 1e-3, t * (1.0 - 0.5 * t), jnp.log2(u) * 0.6931471805599453)
    r = pltpu.reciprocal(u, approx=True)
    return jnp.maximum(pre, 0.0) + log, jnp.where(pre >= 0, r, t * r)


def encode_body(n, tm, fc, *refs):
    parts = refs[:n]
    enc_ref, b_ref, dec_ref, f_ref, s_ref, l_ref, n_ref = refs[n : n + 7]
    tot = None
    counted = 0.0
    at = 0
    for c_ref, p_ref in zip(parts, refs[n + 7 :]):
        for i in range(c_ref.shape[0] // tm):
            rows = slice(at, at + tm)
            at += tm
            c = c_ref[i * tm : (i + 1) * tm, :]
            out = c[:, 0:1].astype(F32) > 0.5 * SENTINEL
            off = jnp.where(out, -1e30, 0.0)
            counted += jnp.sum(jnp.where(out, 0.0, 1.0), axis=0, keepdims=True)
            acc = None
            for k in range(enc_ref.shape[1] // fc):
                sl = slice(k * fc, (k + 1) * fc)
                pre = jnp.dot(c, enc_ref[:, sl], preferred_element_type=F32) + b_ref[:, sl] + off
                feats, sig = activate(pre)
                low = feats.astype(BF)
                f_ref[rows, sl] = low
                s_ref[rows, sl] = sig.astype(BF)
                d = jnp.dot(low, dec_ref[sl, :], preferred_element_type=F32)
                acc = d if acc is None else acc + d
                part = jnp.sum(feats.reshape(-1, 8, fc), axis=0)
                part = sum(part[:, j * 128 : (j + 1) * 128] for j in range(fc // 128))
                tot = part if tot is None else tot + part
            p_ref[i * tm : (i + 1) * tm, :] = acc.astype(p_ref.dtype)
    l_ref[...] = tot
    n_ref[...] = jnp.broadcast_to(counted, n_ref.shape)


def encode(parts, enc, bias, dec, tm=384, fc=768):
    t = sum(c.shape[0] for c in parts)
    d, nf = enc.shape
    outs = [((t, nf), BF), ((t, nf), BF), ((8, 128), F32), ((8, d), F32)] + [(c.shape, BF) for c in parts]
    return local(functools.partial(encode_body, len(parts), tm, fc), outs, (*parts, enc, bias, dec))


def flatten(groups):
    arrays, spec = [], []
    for group in groups:
        spec.append([])
        for part in group:
            spec[-1].append([])
            for v, a, b in part:
                k = next((i for i, w in enumerate(arrays) if w is v), len(arrays))
                if k == len(arrays):
                    arrays.append(v)
                spec[-1][-1].append((k, a, b))
    return arrays, spec


def rows_of(refs, part, lanes=slice(None)):
    blocks = [refs[k][a:b, lanes] for k, a, b in part]
    return blocks[0] if len(blocks) == 1 else jnp.concatenate(blocks, 0)


def grad_dec_body(spec, n, has, start, fb, *refs):
    rest = refs[n:]
    out = rest[-1]
    for k in range(out.shape[0] // fb):
        sl = slice(start + k * fb, start + (k + 1) * fb)
        acc = rest[0][sl, :] if has else None
        for f, g in spec:
            d = lax.dot_general(rows_of(refs, f, sl), rows_of(refs, g), TN, preferred_element_type=F32)
            acc = d if acc is None else acc + d
        out[k * fb : (k + 1) * fb, :] = acc.astype(out.dtype)


def grad_dec(groups, acc, dtype, shape, start=0, size=None, fb=768):
    arrays, spec = flatten(groups)
    n = len(arrays)
    nf, d = shape
    size = nf if size is None else size
    has = acc is not None
    return local(
        functools.partial(grad_dec_body, spec, n, has, start, fb),
        [((size, d), dtype)],
        (*arrays, *([acc] * has)),
        aliases={n: 0} if has and dtype == F32 else {},
    )[0]


def grad_enc_body(spec, n, has, start, fb, *refs):
    dec, rest = refs[n], refs[n + 1 :]
    out, out_tot = rest[-2:]
    for k in range(out.shape[1] // fb):
        sl = slice(start + k * fb, start + (k + 1) * fb)
        ol = slice(k * fb, (k + 1) * fb)
        acc = rest[0][:, sl] if has else None
        tot = rest[1][:, sl] if has else None
        for s, g, c in spec:
            gf = lax.dot_general(rows_of(refs, g), dec[sl, :], NT, preferred_element_type=F32)
            gp = (gf + sparsity_cost) * rows_of(refs, s, sl).astype(F32)
            part = jnp.sum(gp, axis=0, keepdims=True)
            tot = part if tot is None else tot + part
            d = lax.dot_general(rows_of(refs, c), gp.astype(BF), TN, preferred_element_type=F32)
            acc = d if acc is None else acc + d
        out[:, ol] = acc.astype(out.dtype)
        out_tot[:, ol] = tot


def grad_enc(groups, dec, acc, tot, dtype, start=0, size=None, fb=768):
    arrays, spec = flatten(groups)
    n = len(arrays)
    nf, d = dec.shape
    size = nf if size is None else size
    has = acc is not None
    outs = [((d, size), dtype), ((1, size), F32)]
    aliases = {n + 1: 0, n + 2: 1} if has and dtype == F32 else {}
    args = (*arrays, dec, *([acc, tot] if has else []))
    return local(functools.partial(grad_enc_body, spec, n, has, start, fb), outs, args, aliases=aliases)


def split_body(bit_ref, *refs):
    send, keep = refs[-2:]
    rows = keep.shape[0]
    here = pl.multiple_of(bit_ref[0] * rows, rows)
    there = pl.multiple_of((1 - bit_ref[0]) * rows, rows)
    send[...] = sum(r[pl.ds(there, rows), :].astype(F32) for r in refs[:-2]).astype(BF)
    keep[...] = sum(r[pl.ds(here, rows), :].astype(F32) for r in refs[:-2])


def split_sum(arrays, bit):
    rows, d = arrays[0].shape
    return local(split_body, [((rows // 2, d), BF), ((rows // 2, d), F32)], arrays, (bit,))


def count_body(n_ref, out_ref, packed_ref):
    out_ref[...] = n_ref[...]
    packed_ref[...] = pack(n_ref[...])


def split_few_body(bit_ref, a_ref, got_ref, few_ref, send, keep, few_out):
    rows = keep.shape[0]
    here = pl.multiple_of(bit_ref[0] * rows, rows)
    there = pl.multiple_of((1 - bit_ref[0]) * rows, rows)
    few = few_ref[...] + unpack(got_ref[2 * rows :, :])
    few_out[...] = few
    sent = a_ref[pl.ds(there, rows), :].astype(F32) + got_ref[pl.ds(there, rows), :].astype(F32)
    send[:rows, :] = sent.astype(BF)
    send[rows:, :] = pack(few)
    keep[...] = a_ref[pl.ds(here, rows), :].astype(F32) + got_ref[pl.ds(here, rows), :].astype(F32)


def split_few(mine, got, few, bit):
    rows, d = mine.shape
    h = rows // 2
    outs = [((h + 16, d), BF), ((h, d), F32), (few.shape, F32)]
    return local(split_few_body, outs, (mine, got, few), (bit,))


def split_pair_body(bit_ref, a_ref, got_ref, few_ref, few_got_ref, send, keep, few_out):
    rows = keep.shape[0]
    here = pl.multiple_of(bit_ref[0] * rows, rows)
    there = pl.multiple_of((1 - bit_ref[0]) * rows, rows)
    few = few_ref[...] + few_got_ref[...]
    few_out[...] = few
    sent = a_ref[pl.ds(there, rows), :].astype(F32) + got_ref[pl.ds(there, rows), :].astype(F32)
    send[:rows, :] = sent.astype(BF)
    send[rows:, :] = pack(few)
    keep[...] = a_ref[pl.ds(here, rows), :].astype(F32) + got_ref[pl.ds(here, rows), :].astype(F32)


def split_pair(mine, got, few, few_got, bit):
    rows, d = mine.shape
    h = rows // 2
    outs = [((h + 16, d), BF), ((h, d), F32), (few.shape, F32)]
    return local(split_pair_body, outs, (mine, got, few, few_got), (bit,))


def total_few_body(a_ref, got_ref, few_ref, out_ref, few_out):
    rows = a_ref.shape[0]
    out_ref[...] = (a_ref[...] + got_ref[:rows, :].astype(F32)).astype(BF)
    few_out[...] = few_ref[...] + unpack(got_ref[rows:, :])


def total_few(keep, got, few):
    return local(total_few_body, [(keep.shape, BF), (few.shape, F32)], (keep, got, few))


def bias_body(along_ref, few_ref, n_ref, *refs):
    row = lax.broadcasted_iota(jnp.int32, few_ref.shape, 0)
    few = jnp.where(row == 2, few_ref[...], along_ref[...])
    scale = 1.0 / n_ref[:1, :1]
    outs = refs[6:]
    for k, (row, rate) in enumerate(((2, 2.0), (0, 0.1))):
        master, moment, average = (r[...][None, :] for r in refs[3 * k : 3 * k + 3])
        made = advance(master, moment, average, few[row : row + 1, :] * scale, rate, False)
        for out, v in zip(outs[3 * k : 3 * k + 3], made):
            out[...] = v[0]
    outs[6][...] = few[1:2, :1]
    outs[7][...] = n_ref[:1, :1]


def bias_update(along, few, count, enc, dec):
    vmem = pl.BlockSpec(memory_space=pltpu.VMEM)
    return pl.pallas_call(
        bias_body,
        in_specs=[vmem] * 9,
        out_specs=[vmem] * 8,
        out_shape=[jax.ShapeDtypeStruct(v.shape, F32) for v in (*enc, *dec)] + [jax.ShapeDtypeStruct((1, 1), F32)] * 2,
        compiler_params=pltpu.CompilerParams(vmem_limit_bytes=4 * 2**20),
        cost_estimate=COST,
    )(along, few, count, *enc, *dec)


def update_body(rate, rows_unit, order_ref, n_ref, g_ref, w_ref, m_ref, a_ref, *refs):
    w_out, m_out, a_out = refs[-3:]
    g = g_ref[...].astype(F32) * (1.0 / n_ref[:1, :1])
    w_out[...], m_out[...], a_out[...] = advance(w_ref[...], m_ref[...], a_ref[...], g, rate, rows_unit)


def update(g, order, count, weights, rate, rows_unit, made=None):
    q, d = weights[0].shape[0] // 4, g.shape[1]
    there = pl.BlockSpec((q, d), lambda i, order: (order[i], 0))
    return pl.pallas_call(
        functools.partial(update_body, rate, rows_unit),
        grid_spec=pltpu.PrefetchScalarGridSpec(
            num_scalar_prefetch=1,
            grid=(2,),
            in_specs=[
                pl.BlockSpec((8, d), lambda i, order: (0, 0)),
                pl.BlockSpec((q, d), lambda i, order: (i, 0)),
                there,
                there,
                there,
            ]
            + ([pl.BlockSpec(memory_space=pl.ANY)] * 3 if made else []),
            out_specs=[there] * 3,
        ),
        out_shape=[jax.ShapeDtypeStruct(weights[0].shape, F32)] * 3,
        input_output_aliases={6: 0, 7: 1, 8: 2} if made else {},
        compiler_params=pltpu.CompilerParams(dimension_semantics=("arbitrary",), vmem_limit_bytes=14 * 2**20),
        cost_estimate=COST,
    )(
        order,
        count,
        pltpu.with_memory_space_constraint(g, pltpu.VMEM),
        *weights,
        *(made or []),
    )


def advance(master, moment, average, grad, rate, rows_unit):
    moment_new = momentum_rate * moment + grad
    master_new = master - rate * (grad + momentum_rate * moment_new)
    if rows_unit:
        master_new = master_new * lax.rsqrt(jnp.sum(master_new * master_new, axis=1, keepdims=True) + 1e-06)
    return (master_new, moment_new, average_rate * average + (1.0 - average_rate) * master_new)


def on_device(
    acts,
    valid,
    enc_master,
    enc_bias,
    dec_master,
    dec_bias,
    enc_moment,
    enc_bias_moment,
    dec_moment,
    dec_bias_moment,
    enc_average,
    enc_bias_average,
    dec_average,
    dec_bias_average,
):
    q, width = acts.shape
    heads = width // HEAD
    z = lax.axis_index("dp")
    core = lax.rem(lax.axis_index("feat"), 2)
    high = z // 2
    mixed = lax.rem(z + high, 2)
    bit_1 = jnp.where(core == 0, mixed, high)
    bit_2 = jnp.where(core == 0, high, mixed)
    bit_1 = bit_1.astype(jnp.int32)[None]
    bit_2 = bit_2.astype(jnp.int32)[None]
    valid_row = valid[None]
    bias_row = dec_bias[None]
    order_1 = jnp.concatenate([bit_1 * 2 + bit_2, bit_1 * 2 + 1 - bit_2])
    order_2 = jnp.concatenate([(1 - bit_1) * 2 + bit_2, (1 - bit_1) * 2 + 1 - bit_2])
    acts = after(acts, bit_1, bit_2, order_1, order_2)
    centered = center(acts, valid, dec_bias)

    n = enc_master.shape[1]
    both = jnp.concatenate([enc_master.astype(BF), dec_master.astype(BF)], 0)
    weights = {}

    def first_group(own):
        other = swap(after(both, own), 1)
        weights["enc"] = jnp.concatenate([both[:width], other[:width]], 1)
        weights["dec"] = jnp.concatenate([both[width:], other[width:]], 0)
        weights["bias"] = jnp.concatenate([enc_bias, swap(after(enc_bias, own), 1)], 0)[None, :]
        weights["made"] = encode([own], weights["enc"], weights["bias"], weights["dec"])
        return [weights["made"][3]]

    c_own, c_p, c_m, c_top, c_bottom = spread(centered, first_group, True)
    enc_two, dec_two, bias_two = weights["enc"], weights["dec"], weights["bias"]
    h = 2 * q
    f_own, s_own, l_own, n_own, y_own = weights["made"]
    f_t, s_t, l_t, n_t, y_pt, y_mt = encode([c_p[0][:h], c_m[0][:h]], enc_two, bias_two, dec_two)
    rest = after([stack((c_p[0], h, h + q), c_p[1]), stack((c_m[0], h, h + q), c_m[1])], n_t)
    f_b, s_b, l_b, n_b, y_pb, y_mb = encode(rest, enc_two, bias_two, dec_two)
    f_ft, s_ft, l_ft, n_ft, y_ft = encode([after(c_top, n_b)], enc_two, bias_two, dec_two)
    near_t = near_sum(y_own, move(y_pt, OUTER, 3), move(y_mt, OUTER, 1), 0)
    f_fb, s_fb, l_fb, n_fb, y_fb = encode([after(c_bottom, n_ft, near_t)], enc_two, bias_two, dec_two)
    near_b = near_sum(y_own, move(y_pb, OUTER, 3), move(y_mb, OUTER, 1), h)
    far_t = move(y_ft, OUTER, 2)
    far_b = move(y_fb, OUTER, 2)

    count = n_own + n_t + n_b + n_fb + n_ft
    sparse = l_own + l_t + l_b + l_fb + l_ft

    mine, to_p = outer_sum(near_t, after(far_t, sparse), F32)
    to_m, to_far = outer_sum(near_b, after(far_b, to_p), BF)
    to_p, to_m = after((to_p, to_m), to_far)
    got = direct_scatter(to_p, to_m, to_far, INNER)
    g_block, few = local(
        error_body,
        [((q, width), BF), ((8, width), F32)],
        (mine, *got[::-1], acts, valid_row, bias_row, sparse),
    )

    def all_rows(*arrays):
        return [(v, 0, v.shape[0]) for v in arrays]

    shape = dec_two.shape
    sums = {}

    def own_grads(own):
        sums["d"] = grad_dec([(all_rows(f_own), all_rows(own))], None, F32, shape)
        sums["e"], e_tot = grad_enc([(all_rows(s_own), all_rows(own), all_rows(c_own))], dec_two, None, None, F32)
        sums["t"] = e_tot
        return e_tot, sums["d"]

    g_own, g_p, g_m, g_top, g_bottom = spread(g_block, own_grads, False)
    d_sum, e_sum, e_tot = sums["d"], sums["e"], sums["t"]
    from_p = [(s_t, 0, h), (s_b, 0, h)], all_rows(*g_p), all_rows(*c_p)
    from_m = [(s_t, h, 2 * h), (s_b, h, 2 * h)], all_rows(*g_m), all_rows(*c_m)
    e_sum, e_tot = grad_enc([from_p, from_m], dec_two, e_sum, e_tot, F32, fb=512)
    g_top, g_bottom = after([g_top, g_bottom], e_tot)

    def e_far(after_what):
        top, bottom = after([g_top, g_bottom], after_what)
        return [(all_rows(s_ft, s_fb), all_rows(top, bottom), all_rows(c_top, c_bottom))]

    def d_groups(after_what):
        p, m, top, bottom = after([g_p, g_m, g_top, g_bottom], after_what)
        return [
            ([(f_t, 0, h), (f_b, 0, h)], all_rows(*p)),
            ([(f_t, h, 2 * h), (f_b, h, 2 * h)], all_rows(*m)),
            (all_rows(f_ft, f_fb), all_rows(top, bottom)),
        ]

    count, count_packed = local(count_body, [(count.shape, F32), ((16, width), BF)], (count,))
    d_other = grad_dec(d_groups(count_packed), d_sum, BF, shape, n, n)
    d_got = swap(d_other, 1)
    e_other, t_other = grad_enc(e_far((e_tot, d_other)), dec_two, e_sum, e_tot, BF, n, n)
    e_got = swap(stack(e_other, count_packed), 1)
    e_mine, t_mine = grad_enc(e_far(t_other), dec_two, e_sum, e_tot, BF, 0, n)
    e_send, e_keep, count = split_few(e_mine, e_got, count, bit_1)

    few, few_other = small_sums(after(few, e_keep), t_mine, t_other, enc_two)
    few_got = swap(few_other, 1)
    d_mine = grad_dec(d_groups(few_other), d_sum, BF, shape, 0, n)
    d_send, d_keep, few = split_pair(d_mine, d_got, few, few_got, bit_1)

    enc_weights = enc_master, enc_moment, enc_average
    dec_weights = dec_master, dec_moment, dec_average
    e_send, e_keep, count = split_few(e_keep, after(trade(e_send, 0), d_send), count, bit_2)
    d_send, d_keep, few = split_few(d_keep, after(trade(d_send, 0), e_send), few, bit_2)
    e_total, count = total_few(e_keep, after(trade(e_send, 1), d_send), count)
    d_total, few = total_few(d_keep, after(trade(d_send, 1), e_total), few)
    e_half = stack(e_total, after(trade(e_total, 1), d_total))
    enc_made = update(e_half, order_1, count, enc_weights, 0.3, False)
    along = ring_total(few, ("x", "x"), enc_made[0])
    d_half = stack(d_total, after(trade(d_total, 1), along))
    dec_made = update(d_half, order_1, count, dec_weights, 0.3, True)
    along = along + after(swap(along, 8), dec_made[0])
    enc_new, enc_moment_new, enc_average_new = update(
        after(trade(e_half, 0), along), order_2, count, enc_weights, 0.3, False, enc_made
    )
    along = along + after(swap(along, 24), enc_new)
    d_near = after(trade(d_half, 0), along)
    (
        enc_bias_new,
        enc_bias_moment_new,
        enc_bias_average_new,
        dec_bias_new,
        dec_bias_moment_new,
        dec_bias_average_new,
        loss_sum,
        total_count,
    ) = bias_update(
        along,
        few,
        count,
        (enc_bias, enc_bias_moment, enc_bias_average),
        (dec_bias, dec_bias_moment, dec_bias_average),
    )
    d_near = after(d_near, loss_sum)
    dec_new, dec_moment_new, dec_average_new = update(d_near, order_2, count, dec_weights, 0.3, True, dec_made)
    loss_sum = jnp.reshape(loss_sum, ())
    count = jnp.reshape(total_count, ())
    return (
        loss_sum,
        count,
        enc_new,
        enc_bias_new,
        dec_new,
        dec_bias_new,
        enc_moment_new,
        enc_bias_moment_new,
        dec_moment_new,
        dec_bias_moment_new,
        enc_average_new,
        enc_bias_average_new,
        dec_average_new,
        dec_bias_average_new,
    )


def solution(mesh):
    placed = (
        P(("dp", "feat"), None),
        P(("dp", "feat")),
        P(None, "feat"),
        P("feat"),
        P("feat", None),
        P(),
        P(None, "feat"),
        P("feat"),
        P("feat", None),
        P(),
        P(None, "feat"),
        P("feat"),
        P("feat", None),
        P(),
    )
    return jax.shard_map(
        on_device,
        mesh=mesh,
        in_specs=placed,
        out_specs=(
            P(),
            P(),
            P(None, "feat"),
            P("feat"),
            P("feat", None),
            P(),
            P(None, "feat"),
            P("feat"),
            P("feat", None),
            P(),
            P(None, "feat"),
            P("feat"),
            P("feat", None),
            P(),
        ),
        check_vma=False,
    )
```
